512 devices in a mesh: row: 32 (over y, x, core), col: 16 (over z).
Axes of the slice: x: 4, y: 4, z: 16, core: 2. Of those that a mesh axis runs over, the one named last changes fastest.
Arguments:
- col_samples: float32 [64, 2, 2048, 128], P('row', None, 'col'), may hold values from -6 to 6
- row_samples: float32 [64, 2, 128, 2048], P('row', None, None, 'col'), may hold values from -6 to 6
- pivot_rows: int32 [64, 128], P('row'), may hold values from 0 to 2047
- rank_blocks: int32 [64], P('row'), may hold values from 1 to 8
- upper_inverse: float32 [2, 2048, 2048], P(None, 'col', 'row'), as said below
- upanel_left: float32 [16, 2, 2048, 128], P('col'), may hold values from -0.125 to 0.125
Outputs:
- panel_right: float32 [64, 2, 128, 2048], P('row', None, None, 'col')
- cores: float32 [64, 16, 2, 128, 128], P('row', 'col')
The draws below stay inside these ranges and needn't reach their ends.
Inputs may be any that keep to these rules, and one draw needn't show every extreme that they name: `rank_blocks`: the tile's rank is 16 times this. `upper_inverse`: zero below the diagonal in both parts.
All inputs are finite; a program needn't handle non-finite values.
Results may differ from the reference program's by a relative error of at most 0.00007.
Values sent between devices are 32-bit elements; how exact they have to be, the bound alone decides.
No kernel may reach another device: no remote copies, remote signals or barrier semaphores. Data moves between devices by JAX's collectives and lax.ppermute only.
A program may use at most 64 MiB of HBM per device.

```python
import jax
import jax.numpy as jnp
from jax import lax

B = 2048
R = 128
RANK_STEP = 16
NT = 64
NJ = 16


def draw_upper_inverse(key, part):
    first_key, second_key = jax.random.split(key)
    base = jax.random.normal(first_key, (2, B, B), jnp.float32)
    rows_index = lax.broadcasted_iota(jnp.int32, (2, B, B), 1)
    cols_index = lax.broadcasted_iota(jnp.int32, (2, B, B), 2)
    component = lax.broadcasted_iota(jnp.int32, (2, B, B), 0)
    upper = jnp.where(cols_index >= rows_index, base * (1.0 / B ** 0.5), 0.0)
    diagonal = jax.random.uniform(second_key, (2, B, B), jnp.float32, 0.5, 1.5)
    on_diagonal = (cols_index == rows_index) & (component == 0)
    return upper + jnp.where(on_diagonal, diagonal, 0.0)


def plant(drawn, rng, low, top_value):
    dims = drawn.shape
    spot = [jax.random.randint(jax.random.fold_in(rng, axis), (), 0, dims[axis]) for axis in range(len(dims))]
    drawn = drawn.at[tuple(spot)].set(low)
    longest = dims.index(max(dims))
    spot[longest] = (spot[longest] + 1) % dims[longest]
    return drawn.at[tuple(spot)].set(top_value)


def block_levels(rng, shape, cuts, least, largest):
    gain = 1.0
    for position, blocks in cuts:
        heights = jax.random.uniform(jax.random.fold_in(jax.random.fold_in(rng, 6), position), (blocks,), jnp.float32, least / len(cuts), largest / len(cuts))
        gain = gain * jnp.repeat(jnp.exp(heights), shape[position] // blocks).reshape((-1,) + (1,) * (len(shape) - 1 - position))
    return gain


def normal_values(rng, dims, deviation, limit, shards=(), kind=jnp.bfloat16):
    values = deviation * jax.random.normal(rng, dims, jnp.float32)
    if shards:
        values = values * block_levels(rng, dims, shards, -0.22, 0.18)
    return jnp.clip(values, -limit, limit).astype(kind)


def setup_inputs(seed: int = 0) -> dict:
    streams_of = jax.random.split(jax.random.key(seed), 7)
    col_samples = normal_values(streams_of[0], (NT, 2, B, R), 1.0, 6.0, ((0, 32), (2, 16)), jnp.float32)
    row_samples = normal_values(streams_of[1], (NT, 2, R, B), 1.0, 6.0, ((0, 32), (3, 16)), jnp.float32)
    pivot_rows = plant(jax.random.randint(streams_of[2], (NT, R), 0, B), jax.random.fold_in(streams_of[2], 1), 0, B - 1).astype(jnp.int32)
    rank_blocks = plant(jax.random.randint(streams_of[3], (NT,), 1, R // RANK_STEP + 1), jax.random.fold_in(streams_of[3], 1), 1, (R // RANK_STEP + 1) - 1).astype(jnp.int32)
    upper_inverse = draw_upper_inverse(jax.random.fold_in(streams_of[6], 71), 0)
    upanel_left = normal_values(streams_of[5], (NJ, 2, B, R), B ** -0.5, 0.125, ((0, 16),), jnp.float32)
    return {"col_samples": col_samples, "row_samples": row_samples, "pivot_rows": pivot_rows, "rank_blocks": rank_blocks, "upper_inverse": upper_inverse, "upanel_left": upanel_left}


def complex_product(pattern, left_real, left_imag, right_real, right_imag):
    def single(left, right):
        return jnp.einsum(pattern, left, right, precision=lax.Precision.HIGHEST, preferred_element_type=jnp.float32)
    real_part = single(left_real, right_real) - single(left_imag, right_imag)
    imag_part = single(left_real, right_imag) + single(left_imag, right_real)
    return real_part, imag_part


def scale_rows(values, weight_real, weight_imag):
    wr = weight_real[:, :, None]
    wi = weight_imag[:, :, None]
    real_part = values[:, 0] * wr - values[:, 1] * wi
    imag_part = values[:, 0] * wi + values[:, 1] * wr
    return jnp.stack((real_part, imag_part), axis=1)


def reference(col_samples, row_samples, pivot_rows, rank_blocks, upper_inverse, upanel_left):
    count = col_samples.shape[0]
    index = jnp.broadcast_to(pivot_rows[:, None, None, :], (count, 2, 1, R)).astype(jnp.int32)
    entries = jnp.take_along_axis(col_samples, index, axis=2)[:, :, 0, :]
    levels = lax.broadcasted_iota(jnp.int32, (1, R), 1)
    keeping = (levels < RANK_STEP * rank_blocks[:, None]).astype(jnp.float32)
    magnitude = jnp.maximum(entries[:, 0] * entries[:, 0] + entries[:, 1] * entries[:, 1], 1.0)
    factor_real = keeping * entries[:, 0] / magnitude
    factor_imag = -keeping * entries[:, 1] / magnitude
    scaled = scale_rows(row_samples, factor_real, factor_imag)
    real_part, imag_part = complex_product("trk,kn->trn", scaled[:, 0], scaled[:, 1], upper_inverse[0], upper_inverse[1])
    panel_right = jnp.stack((real_part, imag_part), axis=1)
    core_real, core_imag = complex_product("trn,jns->tjrs", panel_right[:, 0], panel_right[:, 1], upanel_left[:, 0], upanel_left[:, 1])
    cores = jnp.stack((core_real, core_imag), axis=2)
    return panel_right, cores
```

```python
import jax
import jax.numpy as jnp
from jax import lax
from jax.experimental import pallas as pl
from jax.experimental.pallas import tpu as pltpu
from jax.sharding import Mesh
from jax.sharding import PartitionSpec as P

RANK_STEP = 16
CHIPS = ("y", "x")
SCALE = 2.0 ** -12
UNSCALE = 2.0 ** 12


def params():
    return pltpu.CompilerParams(vmem_limit_bytes=48 * 1024 * 1024)


def cost(flops, moved):
    return pl.CostEstimate(flops=flops, bytes_accessed=moved, transcendentals=0)


def split(x):
    high = x.astype(jnp.bfloat16)
    low = (x - high.astype(jnp.float32)).astype(jnp.bfloat16)
    return high, low


def dot(a, b):
    return jnp.dot(a, b, preferred_element_type=jnp.float32)


def entries_kernel(pivots_ref, cols_ref, out_ref):
    width = cols_ref.shape[2]
    rows = lax.broadcasted_iota(jnp.int32, cols_ref.shape[2:], 0) + lax.axis_index("col") * width
    for i in range(2):
        hit = pivots_ref[i : i + 1, :] == rows
        for p in range(2):
            out_ref[2 * i + p : 2 * i + p + 1, :] = jnp.sum(
                jnp.where(hit, cols_ref[i, p], 0.0), axis=0, keepdims=True
            )


def pack_kernel(own_ref, moved_ref, out_ref):
    chip = lax.axis_index("y") * lax.axis_size("x") + lax.axis_index("x")
    place = lax.axis_index("col")
    swap = jnp.logical_and(chip == 1, place == lax.axis_size("col") - 1)
    core = lax.axis_index("c")
    parts = []
    for p in range(2):
        block = jnp.where(swap, moved_ref[p], own_ref[p])
        parts.append(block.T.reshape(16, 8, 128))
    first = lax.broadcasted_iota(jnp.int32, (16, 8, 128), 1) < 4
    low = jnp.where(first, parts[0], jnp.roll(parts[1], 4, axis=1))
    high = jnp.where(first, jnp.roll(parts[0], 4, axis=1), parts[1])
    out_ref[...] = jnp.where(core == 0, low, high)


def right_kernel(ranks_ref, rows_ref, left_ref, out_ref, factor_ref):
    place = lax.axis_index("col")
    corner = rows_ref[15, 0:8, :]
    total = None
    for q in range(16):
        if q == 0:
            x = jnp.concatenate([corner, jnp.zeros((120, 128), jnp.float32)], axis=0)
        elif q == 1:
            x = jnp.concatenate(
                [rows_ref[0:15, 0:8, :].reshape(120, 128), jnp.zeros((8, 128), jnp.float32)], axis=0
            )
        else:
            x = rows_ref[:, 8 * q - 8 : 8 * q, :].reshape(128, 128)
        y = jnp.concatenate(
            [left_ref[0, 128 * q : 128 * q + 128, :], left_ref[1, 128 * q : 128 * q + 128, :]], axis=1
        )
        xh, xl = split(x)
        yh, yl = split(y * SCALE)
        term = dot(xh, yh) + (dot(xh, yl) + dot(xl, yh))
        total = term if total is None else total + term
    by_real = total[:, :128].reshape(16, 8, 128)
    by_imag = jnp.roll(total[:, 128:].reshape(16, 8, 128), 4, axis=1)
    first = lax.broadcasted_iota(jnp.int32, (16, 8, 128), 1) < 4
    product = by_real + jnp.where(first, -by_imag, by_imag)
    start = pl.multiple_of(jnp.maximum(place - 1, 0) * 8, 8)
    block = rows_ref[:, pl.ds(start, 8), :]
    which = lax.broadcasted_iota(jnp.int32, (16, 8, 128), 0)
    block = jnp.where(jnp.logical_and(place == 1, which == 15), 0.0, block)
    at_zero = jnp.where(which == 0, corner[None], 0.0)
    block = jnp.where(place == 0, at_zero, block)
    for d in range(16):
        out_ref[d, :, 0] = block
        out_ref[d, :, 1] = product
    entries = jnp.sum(rows_ref[:, 120:124, :], axis=0)
    levels = lax.broadcasted_iota(jnp.int32, (1, 128), 1)
    for i in range(2):
        real, imag = entries[2 * i : 2 * i + 1], entries[2 * i + 1 : 2 * i + 2]
        keeping = (levels < RANK_STEP * ranks_ref[i]).astype(jnp.float32)
        magnitude = jnp.maximum(real * real + imag * imag, 1.0)
        factor_ref[2 * i : 2 * i + 1, :] = keeping * real / magnitude
        factor_ref[2 * i + 1 : 2 * i + 2, :] = -keeping * imag / magnitude
    factor_ref[4:8, :] = jnp.zeros((4, 128), jnp.float32)


def left_kernel(factor_ref, rows_ref, out_ref):
    core = lax.axis_index("c")
    columns = factor_ref[...].T
    first = (lax.broadcasted_iota(jnp.int32, (128, 128), 1) & 7) < 4
    for i in range(2):
        wr, wi = columns[:, 2 * i : 2 * i + 1], columns[:, 2 * i + 1 : 2 * i + 2]
        vr, vi = rows_ref[0, i, 0], rows_ref[0, i, 1]
        real, imag = vr * wr - vi * wi, vr * wi + vi * wr
        for p, (a, b) in enumerate(((real, -imag), (imag, real))):
            span = pl.ds(256 * p + 128 * i, 128)
            for slot, v in (
                (core, jnp.where(first, a, pltpu.roll(b, 4, 1))),
                (1 - core, jnp.where(first, pltpu.roll(a, 124, 1), b)),
            ):
                high, low = split(v)
                out_ref[slot, 0, span, :] = high
                out_ref[slot, 1, span, :] = low


def partial_sum(left_ref, right_ref):
    pieces = []
    for z in range(right_ref.shape[1]):
        pieces.append(
            jnp.concatenate(
                [right_ref[:, z, 0].reshape(128, 128), right_ref[:, z, 1].reshape(128, 128)], axis=1
            )
        )
    high, low = split(jnp.concatenate(pieces, axis=0))
    lh, ll = left_ref[0, 0], left_ref[0, 1]
    return dot(lh, high) + (dot(lh, low) + dot(ll, high))


def first_kernel(left_ref, right_ref, out_ref):
    @pl.when(pl.program_id(0) == 0)
    def _():
        out_ref[...] = jnp.zeros_like(out_ref)

    out_ref[...] += partial_sum(left_ref, right_ref)


def second_kernel(left_ref, right_ref, start_ref, panel_ref, cores_ref, total_ref):
    step = pl.program_id(0)

    @pl.when(step == 0)
    def _():
        total_ref[...] = start_ref[...]

    total_ref[...] += partial_sum(left_ref, right_ref)

    @pl.when(step == pl.num_programs(0) - 1)
    def _():
        for i in range(2):
            for p in range(2):
                span = slice(256 * p + 128 * i, 256 * p + 128 * i + 128)
                panel_ref[i, p] = total_ref[span, 0:128]
                cores_ref[i, 0, p] = total_ref[span, 128:256] * UNSCALE


STEPS = 4


def product_call(slot, left, right, start=None):
    depth = 16 // STEPS
    in_specs = [
        pl.BlockSpec((1, 2, 512, 128 * depth), lambda s: (slot, 0, 0, s)),
        pl.BlockSpec((16, depth, 2, 8, 128), lambda s: (0, s, 0, 0, 0)),
    ]
    estimate = cost(2 * 3 * 512 * 2048 * 256, 7 * 1024 * 1024)
    if start is None:
        return pl.pallas_call(
            first_kernel,
            grid=(STEPS,),
            in_specs=in_specs,
            out_specs=pl.BlockSpec((512, 256), lambda s: (0, 0)),
            out_shape=jax.ShapeDtypeStruct((512, 256), jnp.float32),
            compiler_params=params(),
            cost_estimate=estimate,
        )(left, right)
    return pl.pallas_call(
        second_kernel,
        grid=(STEPS,),
        in_specs=in_specs + [pl.BlockSpec((512, 256), lambda s: (0, 0))],
        out_specs=(
            pl.BlockSpec((2, 2, 128, 128), lambda s: (0, 0, 0, 0)),
            pl.BlockSpec((2, 1, 2, 128, 128), lambda s: (0, 0, 0, 0, 0)),
        ),
        out_shape=(
            jax.ShapeDtypeStruct((2, 2, 128, 128), jnp.float32),
            jax.ShapeDtypeStruct((2, 1, 2, 128, 128), jnp.float32),
        ),
        scratch_shapes=[pltpu.VMEM((512, 256), jnp.float32)],
        compiler_params=params(),
        cost_estimate=estimate,
    )(left, right, start)


def on_device(col_samples, row_samples, pivot_rows, rank_blocks, upper_inverse, upanel_left):
    f32 = jnp.float32
    vmem = pl.BlockSpec(memory_space=pltpu.VMEM)
    rows = lax.all_gather(row_samples, "col", axis=0)

    flipped = jnp.swapaxes(upper_inverse, 1, 2)
    flipped = lax.all_gather(flipped, "c", axis=1, tiled=True)
    last = lax.axis_size("col") - 1
    moved = lax.ppermute(
        flipped, CHIPS + ("col",), [(0, 1 * (last + 1) + last)]
    )
    entries = pl.pallas_call(
        entries_kernel,
        in_specs=[vmem, vmem],
        out_specs=vmem,
        out_shape=jax.ShapeDtypeStruct((4, 128), f32),
        compiler_params=params(),
        cost_estimate=cost(2**17, 2**18),
    )(pivot_rows, col_samples)
    packed = pl.pallas_call(
        pack_kernel,
        in_specs=[vmem, vmem],
        out_specs=vmem,
        out_shape=jax.ShapeDtypeStruct((16, 8, 128), f32),
        compiler_params=params(),
        cost_estimate=cost(2**17, 2**18),
    )(flipped, moved)
    packed = lax.all_to_all(packed, CHIPS, 0, 0)
    packed = jnp.concatenate([packed.reshape(128, 128)[8:], entries], axis=0)
    packed = lax.all_gather(packed, "col", axis=0)
    right, factor = pl.pallas_call(
        right_kernel,
        in_specs=[pl.BlockSpec(memory_space=pltpu.SMEM), vmem, vmem],
        out_specs=(vmem, vmem),
        out_shape=(jax.ShapeDtypeStruct((16, 16, 2, 8, 128), f32), jax.ShapeDtypeStruct((8, 128), f32)),
        compiler_params=params(),
        cost_estimate=cost(2 * 3 * 128 * 2048 * 256, 5 * 2**20),
    )(rank_blocks, packed, upanel_left[0])
    own = lax.all_to_all(right, CHIPS, 0, 0)
    left = pl.pallas_call(
        left_kernel,
        grid=(16,),
        in_specs=[
            pl.BlockSpec((8, 128), lambda z: (0, 0)),
            pl.BlockSpec((1, 2, 2, 128, 128), lambda z: (z, 0, 0, 0, 0)),
        ],
        out_specs=pl.BlockSpec((2, 2, 512, 128), lambda z: (0, 0, 0, z)),
        out_shape=jax.ShapeDtypeStruct((2, 2, 512, 2048), jnp.bfloat16),
        compiler_params=params(),
        cost_estimate=cost(2**24, 12 * 2**20),
    )(factor, rows)
    other = lax.ppermute(own, "c", [(0, 1), (1, 0)])
    total = product_call(0, left, own)
    return product_call(1, left, other, total)


def solution(mesh):
    chips = mesh.devices.reshape(4, 4, 2, 16)
    fine = Mesh(chips, ("y", "x", "c", "col"))
    row = ("y", "x", "c")
    in_specs = (
        P(row, None, "col", None),
        P(row, None, None, "col"),
        P(row, None),
        P(row),
        P(None, "col", row),
        P("col", None, None, None),
    )
    out_specs = (P(row, None, None, "col"), P(row, "col", None, None, None))
    return jax.shard_map(
        on_device, mesh=fine, in_specs=in_specs, out_specs=out_specs, check_vma=False
    )
```

```python
import jax
import jax.numpy as jnp
from jax import lax
from jax.experimental import pallas as pl
from jax.experimental.pallas import tpu as pltpu
from jax.sharding import Mesh
from jax.sharding import PartitionSpec as P

RANK_STEP = 16
CHIPS = ("y", "x")
DOWN_INVERSE, UP_INVERSE = 2.0 ** -16, 2.0 ** 16
DOWN_PRODUCT, UP_PRODUCT = 2.0 ** -24, 2.0 ** 24
PAIRS = 8
DEPTH = 2


def params(mebibytes=24):
    return pltpu.CompilerParams(vmem_limit_bytes=mebibytes * 1024 * 1024)


def cost(flops, moved):
    return pl.CostEstimate(flops=flops, bytes_accessed=moved, transcendentals=0)


def split(x):
    high = x.astype(jnp.bfloat16)
    low = (x - high.astype(jnp.float32)).astype(jnp.bfloat16)
    return high, low


def dot(a, b):
    return jnp.dot(a, b, preferred_element_type=jnp.float32)


def entries_kernel(ranks_ref, pivots_ref, cols_ref, out_ref):
    levels = lax.broadcasted_iota(jnp.int32, (1, cols_ref.shape[3]), 1)
    width = cols_ref.shape[2]
    rows = lax.broadcasted_iota(jnp.int32, cols_ref.shape[2:], 0) + lax.axis_index("col") * width
    for i in range(2):
        hit = jnp.logical_and(pivots_ref[i : i + 1, :] == rows, levels < RANK_STEP * ranks_ref[i])
        for p in range(2):
            out_ref[2 * i + p : 2 * i + p + 1, :] = jnp.sum(
                jnp.where(hit, cols_ref[i, p], 0.0), axis=0, keepdims=True
            )


def pack_kernel(own_ref, moved_ref, out_ref):
    chip = lax.axis_index("y") * lax.axis_size("x") + lax.axis_index("x")
    place = lax.axis_index("col")
    swap = jnp.logical_and(chip == 1, place == lax.axis_size("col") - 1)
    core = lax.axis_index("c")
    parts = []
    for p in range(2):
        block = jnp.where(swap, moved_ref[p], own_ref[p])
        parts.append(block.T.reshape(16, 8, 128))
    first = lax.broadcasted_iota(jnp.int32, (16, 8, 128), 1) < 4
    low = jnp.where(first, parts[0], jnp.roll(parts[1], 4, axis=1))
    high = jnp.where(first, jnp.roll(parts[0], 4, axis=1), parts[1])
    out_ref[...] = jnp.where(core == 0, low, high)


def right_kernel(rows_ref, left_ref, out_ref, factor_ref):
    place = lax.axis_index("col")
    corner = rows_ref[15, 0:8, :]
    total = None
    for q in range(16):
        if q == 0:
            x = jnp.concatenate([corner, jnp.zeros((120, 128), jnp.float32)], axis=0)
        elif q == 1:
            x = jnp.concatenate(
                [rows_ref[0:15, 0:8, :].reshape(120, 128), jnp.zeros((8, 128), jnp.float32)], axis=0
            )
        else:
            x = rows_ref[:, 8 * q - 8 : 8 * q, :].reshape(128, 128)
        y = jnp.concatenate(
            [left_ref[0, 128 * q : 128 * q + 128, :], left_ref[1, 128 * q : 128 * q + 128, :]], axis=1
        )
        xh, xl = split(x)
        yh, yl = split(y * DOWN_PRODUCT)
        term = dot(xh, yh) + (dot(xh, yl) + dot(xl, yh))
        total = term if total is None else total + term
    by_real = total[:, :128].reshape(16, 8, 128)
    by_imag = jnp.roll(total[:, 128:].reshape(16, 8, 128), 4, axis=1)
    first = lax.broadcasted_iota(jnp.int32, (16, 8, 128), 1) < 4
    product = by_real + jnp.where(first, -by_imag, by_imag)
    start = pl.multiple_of(jnp.maximum(place - 1, 0) * 8, 8)
    block = rows_ref[:, pl.ds(start, 8), :]
    which = lax.broadcasted_iota(jnp.int32, (16, 8, 128), 0)
    block = jnp.where(jnp.logical_and(place == 1, which == 15), 0.0, block)
    at_zero = jnp.where(which == 0, corner[None], 0.0)
    block = jnp.where(place == 0, at_zero, block)
    lower = lax.broadcasted_iota(jnp.int32, (PAIRS, 8, 128), 1) < 4
    for n, x in enumerate((block * DOWN_INVERSE, product)):
        x = x.reshape(PAIRS, 2, 8, 128)
        even, odd = x[:, 0], x[:, 1]
        real = jnp.where(lower, even, jnp.roll(odd, 4, axis=1))
        imag = jnp.where(lower, jnp.roll(even, 4, axis=1), odd)
        for d in range(16):
            out_ref[d, :, 2 * n] = real
            out_ref[d, :, 2 * n + 1] = imag
    entries = jnp.sum(rows_ref[:, 120:124, :], axis=0)
    for i in range(2):
        real, imag = entries[2 * i : 2 * i + 1], entries[2 * i + 1 : 2 * i + 2]
        magnitude = jnp.maximum(real * real + imag * imag, 1.0)
        factor_ref[2 * i : 2 * i + 1, :] = real / magnitude
        factor_ref[2 * i + 1 : 2 * i + 2, :] = -imag / magnitude
    factor_ref[4:8, :] = jnp.zeros((4, 128), jnp.float32)


def product(own, rows_ref, right_ref, held_ref, sems):
    copies = [pltpu.make_async_copy(rows_ref.at[z], held_ref.at[z], sems.at[z]) for z in range(16)]
    for copy in copies:
        copy.start()
    core = lax.axis_index("c")
    turn = core if own else 1 - core
    shift = jnp.where(turn == 0, 4, 124)
    keep = ((lax.broadcasted_iota(jnp.int32, (128, 128), 1) & 7) < 4) == (turn == 0)
    total = None
    for step in range(PAIRS // DEPTH):
        lefts, rights = [], []
        for n in range(step * DEPTH, step * DEPTH + DEPTH):
            copies[2 * n].wait()
            copies[2 * n + 1].wait()
            blocks = []
            for p in range(2):
                for i in range(2):
                    still = held_ref[2 * n + turn, i, p]
                    moved = pltpu.roll(held_ref[2 * n + 1 - turn, i, p], shift, 1)
                    blocks.append(jnp.where(keep, still, moved))
            lefts.append(jnp.concatenate(blocks, axis=0))
        for block in right_ref(step):
            rights.append(jnp.concatenate([block[:, m].reshape(128, 128) for m in range(4)], axis=1))
        rh, rl = split(jnp.concatenate(rights, axis=0))
        lh, ll = split(jnp.concatenate(lefts, axis=1))
        term = dot(lh, rh) + (dot(lh, rl) + dot(ll, rh))
        total = term if total is None else total + term
    return total


def first_kernel(rows_ref, right_ref, out_ref, held_ref, sems):
    def right(step):
        return [right_ref[:, n] for n in range(step * DEPTH, step * DEPTH + DEPTH)]

    out_ref[...] = product(True, rows_ref, right, held_ref, sems)


def second_kernel(factor_ref, start_ref, rows_ref, right_ref, panel_ref, cores_ref, held_ref, sems, near_ref, near_sems):
    copies = [
        pltpu.make_async_copy(right_ref.at[:, n], near_ref.at[n], near_sems.at[n]) for n in range(PAIRS)
    ]
    for copy in copies:
        copy.start()

    def right(step):
        span = range(step * DEPTH, step * DEPTH + DEPTH)
        for n in span:
            copies[n].wait()
        return [near_ref[n] for n in span]

    total = start_ref[...] + product(False, rows_ref, right, held_ref, sems)
    columns = factor_ref[...].T
    for i in range(2):
        fr, fi = columns[:, 2 * i : 2 * i + 1], columns[:, 2 * i + 1 : 2 * i + 2]
        by_real, by_imag = total[128 * i : 128 * i + 128], total[256 + 128 * i : 384 + 128 * i]
        for n, up in enumerate((UP_INVERSE, UP_PRODUCT)):
            re, im = slice(256 * n, 256 * n + 128), slice(256 * n + 128, 256 * n + 256)
            real = by_real[:, re] - by_imag[:, im]
            imag = by_real[:, im] + by_imag[:, re]
            pair = (fr * real - fi * imag) * up, (fr * imag + fi * real) * up
            for p in range(2):
                if n == 0:
                    panel_ref[i, p] = pair[p]
                else:
                    cores_ref[i, 0, p] = pair[p]


def first_call(rows, right):
    vmem = pl.BlockSpec(memory_space=pltpu.VMEM)
    return pl.pallas_call(
        first_kernel,
        in_specs=[pl.BlockSpec(memory_space=pltpu.HBM), vmem],
        out_specs=vmem,
        out_shape=jax.ShapeDtypeStruct((512, 512), jnp.float32),
        scratch_shapes=[pltpu.VMEM((16, 2, 2, 128, 128), jnp.float32), pltpu.SemaphoreType.DMA((16,))],
        compiler_params=params(48),
        cost_estimate=cost(2 * 3 * 512 * 1024 * 512, 7 * 2**20),
    )(rows, right)


def second_call(factor, start, rows, right):
    vmem = pl.BlockSpec(memory_space=pltpu.VMEM)
    hbm = pl.BlockSpec(memory_space=pltpu.HBM)
    return pl.pallas_call(
        second_kernel,
        in_specs=[vmem, vmem, hbm, hbm],
        out_specs=(vmem, vmem),
        out_shape=(
            jax.ShapeDtypeStruct((2, 2, 128, 128), jnp.float32),
            jax.ShapeDtypeStruct((2, 1, 2, 128, 128), jnp.float32),
        ),
        scratch_shapes=[
            pltpu.VMEM((16, 2, 2, 128, 128), jnp.float32),
            pltpu.SemaphoreType.DMA((16,)),
            pltpu.VMEM((PAIRS, 16, 4, 8, 128), jnp.float32),
            pltpu.SemaphoreType.DMA((PAIRS,)),
        ],
        compiler_params=params(48),
        cost_estimate=cost(2 * 3 * 512 * 1024 * 512, 8 * 2**20),
    )(factor, start, rows, right)


def on_device(col_samples, row_samples, pivot_rows, rank_blocks, upper_inverse, upanel_left):
    f32 = jnp.float32
    vmem = pl.BlockSpec(memory_space=pltpu.VMEM)
    rows = lax.all_gather(row_samples, "col", axis=0)

    flipped = jnp.swapaxes(upper_inverse, 1, 2)
    flipped = lax.all_gather(flipped, "c", axis=1, tiled=True)
    last = lax.axis_size("col") - 1
    moved = lax.ppermute(
        flipped, CHIPS + ("col",), [(0, 1 * (last + 1) + last)]
    )
    entries = pl.pallas_call(
        entries_kernel,
        in_specs=[pl.BlockSpec(memory_space=pltpu.SMEM), vmem, vmem],
        out_specs=vmem,
        out_shape=jax.ShapeDtypeStruct((4, 128), f32),
        compiler_params=params(),
        cost_estimate=cost(2**17, 2**18),
    )(rank_blocks, pivot_rows, col_samples)
    packed = pl.pallas_call(
        pack_kernel,
        in_specs=[vmem, vmem],
        out_specs=vmem,
        out_shape=jax.ShapeDtypeStruct((16, 8, 128), f32),
        compiler_params=params(),
        cost_estimate=cost(2**17, 2**18),
    )(flipped, moved)
    packed = lax.all_to_all(packed, CHIPS, 0, 0)
    packed = jnp.concatenate([packed.reshape(128, 128)[8:], entries], axis=0)
    packed = lax.all_gather(packed, "col", axis=0)
    right, factor = pl.pallas_call(
        right_kernel,
        in_specs=[vmem, vmem],
        out_specs=(vmem, vmem),
        out_shape=(jax.ShapeDtypeStruct((16, PAIRS, 4, 8, 128), f32), jax.ShapeDtypeStruct((8, 128), f32)),
        compiler_params=params(),
        cost_estimate=cost(2 * 3 * 128 * 2048 * 256, 5 * 2**20),
    )(packed, upanel_left[0])
    own = lax.all_to_all(right, CHIPS, 0, 0)
    other = lax.ppermute(own, "c", [(0, 1), (1, 0)])
    return second_call(factor, first_call(rows, own), rows, other)


def solution(mesh):
    chips = mesh.devices.reshape(4, 4, 2, 16)
    fine = Mesh(chips, ("y", "x", "c", "col"))
    row = ("y", "x", "c")
    in_specs = (
        P(row, None, "col", None),
        P(row, None, None, "col"),
        P(row, None),
        P(row),
        P(None, "col", row),
        P("col", None, None, None),
    )
    out_specs = (P(row, None, None, "col"), P(row, "col", None, None, None))
    return jax.shard_map(
        on_device, mesh=fine, in_specs=in_specs, out_specs=out_specs, check_vma=False
    )
```

```python
import jax
import jax.numpy as jnp
from jax import lax
from jax.experimental import pallas as pl
from jax.experimental.pallas import tpu as pltpu
from jax.sharding import Mesh
from jax.sharding import PartitionSpec as P

RANK_STEP = 16
CHIPS = ("y", "x")
DOWN_INVERSE, UP_INVERSE = 2.0 ** -16, 2.0 ** 16
DOWN_PRODUCT, UP_PRODUCT = 2.0 ** -24, 2.0 ** 24
PAIRS = 8
DEPTH = 2


def params(mebibytes=24):
    return pltpu.CompilerParams(vmem_limit_bytes=mebibytes * 1024 * 1024)


def cost(flops, moved):
    return pl.CostEstimate(flops=flops, bytes_accessed=moved, transcendentals=0)


def split(x):
    high = x.astype(jnp.bfloat16)
    low = (x - high.astype(jnp.float32)).astype(jnp.bfloat16)
    return high, low


def dot(a, b):
    return jnp.dot(a, b, preferred_element_type=jnp.float32)


def entries_kernel(ranks_ref, pivots_ref, cols_ref, out_ref):
    levels = lax.broadcasted_iota(jnp.int32, (1, cols_ref.shape[3]), 1)
    width = cols_ref.shape[2]
    rows = lax.broadcasted_iota(jnp.int32, cols_ref.shape[2:], 0) + lax.axis_index("col") * width
    for i in range(2):
        hit = jnp.logical_and(pivots_ref[i : i + 1, :] == rows, levels < RANK_STEP * ranks_ref[i])
        for p in range(2):
            out_ref[2 * i + p : 2 * i + p + 1, :] = jnp.sum(
                jnp.where(hit, cols_ref[i, p], 0.0), axis=0, keepdims=True
            )
    out_ref[4:8, :] = jnp.zeros((4, 128), jnp.float32)


def sublanes(shape):
    return lax.broadcasted_iota(jnp.int32, shape, len(shape) - 2)


def interleave(even, odd):
    row = sublanes(even.shape)

    def turn(x, n):
        return jnp.roll(x, n, axis=x.ndim - 2)

    even2, odd2, even4, odd4, even6, odd6 = (turn(x, n) for n in (2, 4, 6) for x in (even, odd))
    low = jnp.where(row < 2, even, jnp.where(row < 4, odd2, jnp.where(row < 6, even2, odd4)))
    high = jnp.where(row < 2, even4, jnp.where(row < 4, odd6, jnp.where(row < 6, even6, odd)))
    return low, high


def pack_kernel(block_ref, out_ref):
    rows = jnp.concatenate([block_ref[0].T, block_ref[1].T], axis=1).reshape(16, 8, 128)
    low, high = interleave(rows[:8], rows[8:])
    out_ref[0:8] = low
    out_ref[8:16] = high


def straight(x):
    lane = lax.broadcasted_iota(jnp.int32, x.shape, x.ndim - 1)
    same = (sublanes(x.shape) < 4) == (lane < 64)
    return jnp.where(same, x, jnp.roll(jnp.roll(x, 4, axis=x.ndim - 2), 64, axis=x.ndim - 1))


def right_kernel(rows_ref, left_ref, out_ref, factor_ref):
    place = lax.axis_index("col")
    last = rows_ref[0, 120:126, :]
    corner = straight(jnp.concatenate([last[0:2], jnp.zeros((2, 128), jnp.float32), last[2:6]], axis=0))
    total = None
    for q in range(16):
        if q == 0:
            x = jnp.concatenate([corner, jnp.zeros((120, 128), jnp.float32)], axis=0)
        else:
            x = straight(rows_ref[:, 8 * q - 8 : 8 * q, :]).reshape(128, 128)
        y = jnp.concatenate(
            [left_ref[0, 128 * q : 128 * q + 128, :], left_ref[1, 128 * q : 128 * q + 128, :]], axis=1
        )
        xh, xl = split(x)
        yh, yl = split(y * DOWN_PRODUCT)
        term = dot(xh, yh) + (dot(xh, yl) + dot(xl, yh))
        total = term if total is None else total + term
    by_real = total[:, :128].reshape(16, 8, 128)
    by_imag = jnp.roll(total[:, 128:].reshape(16, 8, 128), 4, axis=1)
    product = by_real + jnp.where(sublanes((16, 8, 128)) < 4, -by_imag, by_imag)
    start = pl.multiple_of(jnp.maximum(place - 1, 0) * 8, 8)
    block = straight(rows_ref[:, pl.ds(start, 8), :])
    which = lax.broadcasted_iota(jnp.int32, (16, 8, 128), 0)
    block = jnp.where(place == 0, jnp.where(which == 0, corner[None], 0.0), block)
    for n, x in enumerate((block * DOWN_INVERSE, product)):
        x = x.reshape(PAIRS, 2, 8, 128)
        real, imag = interleave(x[:, 0], x[:, 1])
        for d in range(16):
            out_ref[d, :, 2 * n] = real
            out_ref[d, :, 2 * n + 1] = imag
    entries = jnp.sum(rows_ref[1:16, 120:124, :], axis=0)
    for i in range(2):
        real, imag = entries[2 * i : 2 * i + 1], entries[2 * i + 1 : 2 * i + 2]
        magnitude = jnp.maximum(real * real + imag * imag, 1.0)
        factor_ref[2 * i : 2 * i + 1, :] = real / magnitude
        factor_ref[2 * i + 1 : 2 * i + 2, :] = -imag / magnitude
    factor_ref[4:8, :] = jnp.zeros((4, 128), jnp.float32)


def product(own, rows_ref, right_ref, held_ref, sems):
    copies = [pltpu.make_async_copy(rows_ref.at[z], held_ref.at[z], sems.at[z]) for z in range(16)]
    for copy in copies:
        copy.start()
    core = lax.axis_index("c")
    turn = core if own else 1 - core
    shift = jnp.where(turn == 0, 2, 126)
    keep = ((lax.broadcasted_iota(jnp.int32, (128, 128), 1) & 3) < 2) == (turn == 0)
    first = sublanes((8, 8, 128)) < 4
    total = None
    for step in range(PAIRS // DEPTH):
        lefts, rights = [], []
        for n in range(step * DEPTH, step * DEPTH + DEPTH):
            copies[2 * n].wait()
            copies[2 * n + 1].wait()
            blocks = []
            for p in range(2):
                for i in range(2):
                    still = held_ref[2 * n + turn, i, p]
                    moved = pltpu.roll(held_ref[2 * n + 1 - turn, i, p], shift, 1)
                    blocks.append(jnp.where(keep, still, moved))
            lefts.append(jnp.concatenate(blocks, axis=0))
        for block in right_ref(step):
            columns = []
            for m in range(4):
                low, high = block[0:8, m], block[8:16, m]
                tiles = (
                    jnp.where(first, low, jnp.roll(high, 4, axis=1)),
                    jnp.where(first, jnp.roll(low, 4, axis=1), high),
                )
                columns.append(jnp.concatenate(tiles, axis=0).reshape(128, 128))
            rights.append(jnp.concatenate(columns, axis=1))
        rh, rl = split(jnp.concatenate(rights, axis=0))
        lh, ll = split(jnp.concatenate(lefts, axis=1))
        term = dot(lh, rh) + (dot(lh, rl) + dot(ll, rh))
        total = term if total is None else total + term
    return total


def first_kernel(rows_ref, right_ref, out_ref, held_ref, sems):
    def right(step):
        return [right_ref[:, n] for n in range(step * DEPTH, step * DEPTH + DEPTH)]

    out_ref[...] = product(True, rows_ref, right, held_ref, sems)


def second_kernel(factor_ref, start_ref, rows_ref, right_ref, panel_ref, cores_ref, held_ref, sems, near_ref, near_sems):
    copies = [
        pltpu.make_async_copy(right_ref.at[:, n], near_ref.at[n], near_sems.at[n]) for n in range(PAIRS)
    ]
    for copy in copies:
        copy.start()

    def right(step):
        span = range(step * DEPTH, step * DEPTH + DEPTH)
        for n in span:
            copies[n].wait()
        return [near_ref[n] for n in span]

    total = start_ref[...] + product(False, rows_ref, right, held_ref, sems)
    columns = factor_ref[...].T
    for i in range(2):
        fr, fi = columns[:, 2 * i : 2 * i + 1], columns[:, 2 * i + 1 : 2 * i + 2]
        by_real, by_imag = total[128 * i : 128 * i + 128], total[256 + 128 * i : 384 + 128 * i]
        for n, up in enumerate((UP_INVERSE, UP_PRODUCT)):
            re, im = slice(256 * n, 256 * n + 128), slice(256 * n + 128, 256 * n + 256)
            real = by_real[:, re] - by_imag[:, im]
            imag = by_real[:, im] + by_imag[:, re]
            pair = (fr * real - fi * imag) * up, (fr * imag + fi * real) * up
            for p in range(2):
                if n == 0:
                    panel_ref[i, p] = pair[p]
                else:
                    cores_ref[i, 0, p] = pair[p]


def first_call(rows, right):
    vmem = pl.BlockSpec(memory_space=pltpu.VMEM)
    return pl.pallas_call(
        first_kernel,
        in_specs=[pl.BlockSpec(memory_space=pltpu.HBM), vmem],
        out_specs=vmem,
        out_shape=jax.ShapeDtypeStruct((512, 512), jnp.float32),
        scratch_shapes=[pltpu.VMEM((16, 2, 2, 128, 128), jnp.float32), pltpu.SemaphoreType.DMA((16,))],
        compiler_params=params(48),
        cost_estimate=cost(2 * 3 * 512 * 1024 * 512, 7 * 2**20),
    )(rows, right)


def second_call(factor, start, rows, right):
    vmem = pl.BlockSpec(memory_space=pltpu.VMEM)
    hbm = pl.BlockSpec(memory_space=pltpu.HBM)
    return pl.pallas_call(
        second_kernel,
        in_specs=[vmem, vmem, hbm, hbm],
        out_specs=(vmem, vmem),
        out_shape=(
            jax.ShapeDtypeStruct((2, 2, 128, 128), jnp.float32),
            jax.ShapeDtypeStruct((2, 1, 2, 128, 128), jnp.float32),
        ),
        scratch_shapes=[
            pltpu.VMEM((16, 2, 2, 128, 128), jnp.float32),
            pltpu.SemaphoreType.DMA((16,)),
            pltpu.VMEM((PAIRS, 16, 4, 8, 128), jnp.float32),
            pltpu.SemaphoreType.DMA((PAIRS,)),
        ],
        compiler_params=params(48),
        cost_estimate=cost(2 * 3 * 512 * 1024 * 512, 8 * 2**20),
    )(factor, start, rows, right)


def on_device(col_samples, row_samples, pivot_rows, rank_blocks, upper_inverse, upanel_left):
    f32 = jnp.float32
    vmem = pl.BlockSpec(memory_space=pltpu.VMEM)
    rows = lax.all_gather(row_samples, "col", axis=0)

    packed = pl.pallas_call(
        pack_kernel,
        in_specs=[vmem],
        out_specs=vmem,
        out_shape=jax.ShapeDtypeStruct((16, 8, 128), f32),
        compiler_params=params(),
        cost_estimate=cost(2**17, 2**18),
    )(jnp.swapaxes(upper_inverse, 1, 2))
    packed = lax.all_to_all(packed.reshape(32, 4, 128), CHIPS + ("c",), 0, 0).reshape(128, 128)
    entries = pl.pallas_call(
        entries_kernel,
        in_specs=[pl.BlockSpec(memory_space=pltpu.SMEM), vmem, vmem],
        out_specs=vmem,
        out_shape=jax.ShapeDtypeStruct((8, 128), f32),
        compiler_params=params(),
        cost_estimate=cost(2**17, 2**18),
    )(rank_blocks, pivot_rows, col_samples)
    place, last = lax.axis_index("col"), lax.axis_size("col") - 1
    entries = entries + lax.ppermute(entries, "col", [(0, last)])
    ends = jnp.concatenate([packed[0:2], packed[4:8]], axis=0)
    packed = jnp.concatenate([packed[8:], jnp.where(place == 0, ends, entries[:6])], axis=0)
    packed = lax.all_gather(packed, "col", axis=0)
    right, factor = pl.pallas_call(
        right_kernel,
        in_specs=[vmem, vmem],
        out_specs=(vmem, vmem),
        out_shape=(jax.ShapeDtypeStruct((16, PAIRS, 4, 8, 128), f32), jax.ShapeDtypeStruct((8, 128), f32)),
        compiler_params=params(),
        cost_estimate=cost(2 * 3 * 128 * 2048 * 256, 5 * 2**20),
    )(packed, upanel_left[0])
    own = lax.all_to_all(right, CHIPS, 0, 0)
    other = lax.ppermute(own, "c", [(0, 1), (1, 0)])
    return second_call(factor, first_call(rows, own), rows, other)


def solution(mesh):
    chips = mesh.devices.reshape(4, 4, 2, 16)
    fine = Mesh(chips, ("y", "x", "c", "col"))
    row = ("y", "x", "c")
    in_specs = (
        P(row, None, "col", None),
        P(row, None, None, "col"),
        P(row, None),
        P(row),
        P(None, "col", row),
        P("col", None, None, None),
    )
    out_specs = (P(row, None, None, "col"), P(row, "col", None, None, None))
    return jax.shard_map(
        on_device, mesh=fine, in_specs=in_specs, out_specs=out_specs, check_vma=False
    )
```

```python
import jax
import jax.numpy as jnp
from jax import lax
from jax.experimental import pallas as pl
from jax.experimental.pallas import tpu as pltpu
from jax.sharding import Mesh
from jax.sharding import PartitionSpec as P

RANK_STEP = 16
CHIPS = ("y", "x")
DOWN_INVERSE, UP_INVERSE = 2.0 ** -16, 2.0 ** 16
DOWN_PRODUCT, UP_PRODUCT = 2.0 ** -24, 2.0 ** 24
PAIRS = 8
DEPTH = 2


def params(mebibytes=24):
    return pltpu.CompilerParams(vmem_limit_bytes=mebibytes * 1024 * 1024)


def cost(flops, moved):
    return pl.CostEstimate(flops=flops, bytes_accessed=moved, transcendentals=0)


def split(x):
    high = x.astype(jnp.bfloat16)
    low = (x - high.astype(jnp.float32)).astype(jnp.bfloat16)
    return high, low


def dot(a, b):
    return jnp.dot(a, b, preferred_element_type=jnp.float32)


def sublanes(shape):
    return lax.broadcasted_iota(jnp.int32, shape, len(shape) - 2)


def interleave(even, odd):
    row = sublanes(even.shape)

    def turn(x, n):
        return jnp.roll(x, n, axis=x.ndim - 2)

    even2, odd2, even4, odd4, even6, odd6 = (turn(x, n) for n in (2, 4, 6) for x in (even, odd))
    low = jnp.where(row < 2, even, jnp.where(row < 4, odd2, jnp.where(row < 6, even2, odd4)))
    high = jnp.where(row < 2, even4, jnp.where(row < 4, odd6, jnp.where(row < 6, even6, odd)))
    return low, high


def start_kernel(block_hbm, cols_hbm, pivots_hbm, ranks_hbm, out_ref, entries_ref, block_ref, cols_ref, pivots_ref, ranks_ref, sems):
    pairs = ((block_hbm, block_ref), (cols_hbm, cols_ref), (pivots_hbm, pivots_ref), (ranks_hbm, ranks_ref))
    copies = [pltpu.make_async_copy(a, b, sems.at[n]) for n, (a, b) in enumerate(pairs)]
    for copy in copies:
        copy.start()
    copies[0].wait()
    rows = jnp.concatenate([block_ref[0].T, block_ref[1].T], axis=1).reshape(16, 8, 128)
    low, high = interleave(rows[:8], rows[8:])
    out_ref[0:8] = low
    out_ref[8:16] = high
    for copy in copies[1:]:
        copy.wait()
    width = cols_ref.shape[2]
    levels = lax.broadcasted_iota(jnp.int32, (1, cols_ref.shape[3]), 1)
    rows = lax.broadcasted_iota(jnp.int32, cols_ref.shape[2:], 0) + lax.axis_index("col") * width
    for i in range(2):
        hit = jnp.logical_and(pivots_ref[i : i + 1, :] == rows, levels < RANK_STEP * ranks_ref[i])
        for p in range(2):
            entries_ref[2 * i + p : 2 * i + p + 1, :] = jnp.sum(
                jnp.where(hit, cols_ref[i, p], 0.0), axis=0, keepdims=True
            )
    entries_ref[4:8, :] = jnp.zeros((4, 128), jnp.float32)


def straight(x):
    lane = lax.broadcasted_iota(jnp.int32, x.shape, x.ndim - 1)
    same = (sublanes(x.shape) < 4) == (lane < 64)
    return jnp.where(same, x, jnp.roll(jnp.roll(x, 4, axis=x.ndim - 2), 64, axis=x.ndim - 1))


def right_kernel(rows_ref, left_ref, out_ref, factor_ref):
    place = lax.axis_index("col")
    last = rows_ref[0, 120:126, :]
    corner = straight(jnp.concatenate([last[0:2], jnp.zeros((2, 128), jnp.float32), last[2:6]], axis=0))
    total = None
    for q in range(16):
        if q == 0:
            x = jnp.concatenate([corner, jnp.zeros((120, 128), jnp.float32)], axis=0)
        else:
            x = straight(rows_ref[:, 8 * q - 8 : 8 * q, :]).reshape(128, 128)
        y = jnp.concatenate(
            [left_ref[0, 128 * q : 128 * q + 128, :], left_ref[1, 128 * q : 128 * q + 128, :]], axis=1
        )
        xh, xl = split(x)
        yh, yl = split(y * DOWN_PRODUCT)
        term = dot(xh, yh) + (dot(xh, yl) + dot(xl, yh))
        total = term if total is None else total + term
    by_real = total[:, :128].reshape(16, 8, 128)
    by_imag = jnp.roll(total[:, 128:].reshape(16, 8, 128), 4, axis=1)
    product = by_real + jnp.where(sublanes((16, 8, 128)) < 4, -by_imag, by_imag)
    start = pl.multiple_of(jnp.maximum(place - 1, 0) * 8, 8)
    block = straight(rows_ref[:, pl.ds(start, 8), :])
    which = lax.broadcasted_iota(jnp.int32, (16, 8, 128), 0)
    block = jnp.where(place == 0, jnp.where(which == 0, corner[None], 0.0), block)
    for n, x in enumerate((block * DOWN_INVERSE, product)):
        x = x.reshape(PAIRS, 2, 8, 128)
        real, imag = interleave(x[:, 0], x[:, 1])
        for d in range(16):
            out_ref[d, :, 2 * n] = real
            out_ref[d, :, 2 * n + 1] = imag
    entries = jnp.sum(rows_ref[1:16, 120:124, :], axis=0)
    for i in range(2):
        real, imag = entries[2 * i : 2 * i + 1], entries[2 * i + 1 : 2 * i + 2]
        magnitude = jnp.maximum(real * real + imag * imag, 1.0)
        factor_ref[2 * i : 2 * i + 1, :] = real / magnitude
        factor_ref[2 * i + 1 : 2 * i + 2, :] = -imag / magnitude
    factor_ref[4:8, :] = jnp.zeros((4, 128), jnp.float32)


def tiles(block):
    first = sublanes((8, 8, 128)) < 4
    low, high = block[0:8], block[8:16]
    pair = (jnp.where(first, low, jnp.roll(high, 4, axis=1)), jnp.where(first, jnp.roll(low, 4, axis=1), high))
    return jnp.concatenate(pair, axis=0).reshape(128, 128)


def dot3(left_high, left_low, right):
    high, low = split(right)
    return dot(left_high, high) + (dot(left_high, low) + dot(left_low, high))


def first_kernel(rows_ref, right_ref, out_ref, later_ref, held_ref, sems):
    copies = [pltpu.make_async_copy(rows_ref.at[z], held_ref.at[z], sems.at[z]) for z in range(16)]
    for copy in copies:
        copy.start()
    core = lax.axis_index("c")
    shift = jnp.where(core == 0, 2, 126)
    keep = ((lax.broadcasted_iota(jnp.int32, (128, 128), 1) & 3) < 2) == (core == 0)
    total = None
    for step in range(PAIRS // DEPTH):
        lefts, rights = [], []
        for n in range(step * DEPTH, step * DEPTH + DEPTH):
            copies[2 * n].wait()
            copies[2 * n + 1].wait()
            blocks = []
            for p in range(2):
                for i in range(2):
                    near, far = held_ref[2 * n + core, i, p], held_ref[2 * n + 1 - core, i, p]
                    blocks.append(jnp.where(keep, near, pltpu.roll(far, shift, 1)))
                    high, low = split(jnp.where(keep, pltpu.roll(near, 128 - shift, 1), far))
                    span = slice(256 * p + 128 * i, 256 * p + 128 * i + 128)
                    later_ref[0, span, 128 * n : 128 * n + 128] = high
                    later_ref[1, span, 128 * n : 128 * n + 128] = low
            lefts.append(jnp.concatenate(blocks, axis=0))
            rights.append(jnp.concatenate([tiles(right_ref[:, n, m]) for m in range(4)], axis=1))
        high, low = split(jnp.concatenate(lefts, axis=1))
        term = dot3(high, low, jnp.concatenate(rights, axis=0))
        total = term if total is None else total + term
    out_ref[...] = total


def second_kernel(
    factor_ref, start_ref, left_ref, right_ref, panel_ref, cores_ref, near_ref, panel_vmem, cores_vmem, sems, out_sems
):
    copies = [
        pltpu.make_async_copy(right_ref.at[:, :, 2 * n : 2 * n + 2], near_ref.at[n], sems.at[n]) for n in range(2)
    ]
    for copy in copies:
        copy.start()
    columns = factor_ref[...].T
    results = (
        (pltpu.make_async_copy(panel_vmem, panel_ref, out_sems.at[0]), panel_vmem, UP_INVERSE),
        (pltpu.make_async_copy(cores_vmem, cores_ref, out_sems.at[1]), cores_vmem, UP_PRODUCT),
    )
    for n, (result, out, up) in enumerate(results):
        copies[n].wait()
        right = jnp.concatenate(
            [
                jnp.concatenate([tiles(near_ref[n, :, z, p]) for p in range(2)], axis=1)
                for z in range(PAIRS)
            ],
            axis=0,
        )
        total = start_ref[:, 256 * n : 256 * n + 256] + dot3(left_ref[0], left_ref[1], right)
        for i in range(2):
            fr, fi = columns[:, 2 * i : 2 * i + 1], columns[:, 2 * i + 1 : 2 * i + 2]
            by_real, by_imag = total[128 * i : 128 * i + 128], total[256 + 128 * i : 384 + 128 * i]
            real = by_real[:, :128] - by_imag[:, 128:]
            imag = by_real[:, 128:] + by_imag[:, :128]
            where = (i,) if n == 0 else (i, 0)
            out[where + (0,)] = (fr * real - fi * imag) * up
            out[where + (1,)] = (fr * imag + fi * real) * up
        result.start()
    for result, _, _ in results:
        result.wait()


def first_call(rows, right):
    vmem = pl.BlockSpec(memory_space=pltpu.VMEM)
    return pl.pallas_call(
        first_kernel,
        in_specs=[pl.BlockSpec(memory_space=pltpu.HBM), vmem],
        out_specs=(vmem, vmem),
        out_shape=(
            jax.ShapeDtypeStruct((512, 512), jnp.float32),
            jax.ShapeDtypeStruct((2, 512, 1024), jnp.bfloat16),
        ),
        scratch_shapes=[pltpu.VMEM((16, 2, 2, 128, 128), jnp.float32), pltpu.SemaphoreType.DMA((16,))],
        compiler_params=params(48),
        cost_estimate=cost(2 * 3 * 512 * 1024 * 512, 7 * 2**20),
    )(rows, right)


def second_call(factor, start, left, right):
    vmem = pl.BlockSpec(memory_space=pltpu.VMEM)
    hbm = pl.BlockSpec(memory_space=pltpu.HBM)
    shapes = (2, 2, 128, 128), (2, 1, 2, 128, 128)
    return pl.pallas_call(
        second_kernel,
        in_specs=[vmem, vmem, vmem, hbm],
        out_specs=(hbm, hbm),
        out_shape=tuple(jax.ShapeDtypeStruct(shape, jnp.float32) for shape in shapes),
        scratch_shapes=[
            pltpu.VMEM((2, 16, PAIRS, 2, 8, 128), jnp.float32),
            pltpu.VMEM(shapes[0], jnp.float32),
            pltpu.VMEM(shapes[1], jnp.float32),
            pltpu.SemaphoreType.DMA((2,)),
            pltpu.SemaphoreType.DMA((2,)),
        ],
        compiler_params=params(48),
        cost_estimate=cost(2 * 3 * 512 * 1024 * 512, 8 * 2**20),
    )(factor, start, left, right)


def on_device(col_samples, row_samples, pivot_rows, rank_blocks, upper_inverse, upanel_left):
    f32 = jnp.float32
    vmem = pl.BlockSpec(memory_space=pltpu.VMEM)
    rows = lax.all_gather(row_samples, "col", axis=0)

    hbm = pl.BlockSpec(memory_space=pltpu.HBM)
    packed, entries = pl.pallas_call(
        start_kernel,
        in_specs=[hbm] * 4,
        out_specs=(vmem, vmem),
        out_shape=(jax.ShapeDtypeStruct((16, 8, 128), f32), jax.ShapeDtypeStruct((8, 128), f32)),
        scratch_shapes=[
            pltpu.VMEM((2, 64, 128), f32),
            pltpu.VMEM(col_samples.shape, f32),
            pltpu.VMEM(pivot_rows.shape, jnp.int32),
            pltpu.SMEM(rank_blocks.shape, jnp.int32),
            pltpu.SemaphoreType.DMA((4,)),
        ],
        compiler_params=params(48),
        cost_estimate=cost(2**17, 2**18),
    )(jnp.swapaxes(upper_inverse, 1, 2), col_samples, pivot_rows, rank_blocks)
    packed = lax.all_to_all(packed.reshape(32, 4, 128), CHIPS + ("c",), 0, 0).reshape(128, 128)
    place, last = lax.axis_index("col"), lax.axis_size("col") - 1
    entries = entries + lax.ppermute(entries, "col", [(0, last)])
    ends = jnp.concatenate([packed[0:2], packed[4:8]], axis=0)
    packed = jnp.concatenate([packed[8:], jnp.where(place == 0, ends, entries[:6])], axis=0)
    packed = lax.all_gather(packed, "col", axis=0)
    right, factor = pl.pallas_call(
        right_kernel,
        in_specs=[vmem, vmem],
        out_specs=(vmem, vmem),
        out_shape=(jax.ShapeDtypeStruct((16, PAIRS, 4, 8, 128), f32), jax.ShapeDtypeStruct((8, 128), f32)),
        compiler_params=params(),
        cost_estimate=cost(2 * 3 * 128 * 2048 * 256, 5 * 2**20),
    )(packed, upanel_left[0])
    own = lax.all_to_all(right, CHIPS, 0, 0)
    other = lax.ppermute(own, "c", [(0, 1), (1, 0)])
    start, left = first_call(rows, own)
    return second_call(factor, start, left, other)


def solution(mesh):
    chips = mesh.devices.reshape(4, 4, 2, 16)
    fine = Mesh(chips, ("y", "x", "c", "col"))
    row = ("y", "x", "c")
    in_specs = (
        P(row, None, "col", None),
        P(row, None, None, "col"),
        P(row, None),
        P(row),
        P(None, "col", row),
        P("col", None, None, None),
    )
    out_specs = (P(row, None, None, "col"), P(row, "col", None, None, None))
    return jax.shard_map(
        on_device, mesh=fine, in_specs=in_specs, out_specs=out_specs, check_vma=False
    )
```

```python
import jax
import jax.numpy as jnp
from jax import lax
from jax.experimental import pallas as pl
from jax.experimental.pallas import tpu as pltpu
from jax.sharding import Mesh
from jax.sharding import PartitionSpec as P

RANK_STEP = 16
CHIPS = ("y", "x")
DOWN_INVERSE, UP_INVERSE = 2.0 ** -16, 2.0 ** 16
DOWN_PRODUCT, UP_PRODUCT = 2.0 ** -24, 2.0 ** 24
PAIRS = 8
DEPTH = 4
ROWS = 512


def params(mebibytes=24):
    return pltpu.CompilerParams(vmem_limit_bytes=int(mebibytes * 2**20))


def cost(flops, moved):
    return pl.CostEstimate(flops=flops, bytes_accessed=moved, transcendentals=0)


def split(x):
    high = x.astype(jnp.bfloat16)
    low = (x - high.astype(jnp.float32)).astype(jnp.bfloat16)
    return high, low


def dot(a, b):
    return jnp.dot(a, b, preferred_element_type=jnp.float32)


def sublanes(shape):
    return lax.broadcasted_iota(jnp.int32, shape, len(shape) - 2)


def interleave(even, odd):
    row = sublanes(even.shape)

    def turn(x, n):
        return jnp.roll(x, n, axis=x.ndim - 2)

    even2, odd2, even4, odd4, even6, odd6 = (turn(x, n) for n in (2, 4, 6) for x in (even, odd))
    low = jnp.where(row < 2, even, jnp.where(row < 4, odd2, jnp.where(row < 6, even2, odd4)))
    high = jnp.where(row < 2, even4, jnp.where(row < 4, odd6, jnp.where(row < 6, even6, odd)))
    return low, high


def start_kernel(
    block_hbm, rows_hbm, cols_hbm, pivots_hbm, ranks_hbm, out_ref, sent_ref, block_ref, cols_ref, pivots_ref, ranks_ref, entries_ref, sems
):
    entries_to = sent_ref.at[ROWS : ROWS + 8]
    pairs = (
        (block_hbm, block_ref),
        (cols_hbm, cols_ref),
        (pivots_hbm, pivots_ref),
        (ranks_hbm, ranks_ref),
        (rows_hbm, sent_ref.at[0:ROWS]),
    )
    copies = [pltpu.make_async_copy(a, b, sems.at[n]) for n, (a, b) in enumerate(pairs)]
    for copy in copies:
        copy.start()
    copies[0].wait()
    rows = jnp.concatenate([block_ref[0].T, block_ref[1].T], axis=1).reshape(16, 8, 128)
    low, high = interleave(rows[:8], rows[8:])
    out_ref[0:8] = low
    out_ref[8:16] = high
    for copy in copies[1:4]:
        copy.wait()
    width = cols_ref.shape[2]
    levels = lax.broadcasted_iota(jnp.int32, (1, cols_ref.shape[3]), 1)
    rows = lax.broadcasted_iota(jnp.int32, cols_ref.shape[2:], 0) + lax.axis_index("col") * width
    for i in range(2):
        hit = jnp.logical_and(pivots_ref[i : i + 1, :] == rows, levels < RANK_STEP * ranks_ref[i])
        for p in range(2):
            entries_ref[2 * i + p : 2 * i + p + 1, :] = jnp.sum(
                jnp.where(hit, cols_ref[i, p], 0.0), axis=0, keepdims=True
            )
    entries_ref[4:8, :] = jnp.zeros((4, 128), jnp.float32)
    last = pltpu.make_async_copy(entries_ref, entries_to, sems.at[5])
    last.start()
    copies[4].wait()
    last.wait()


def straight(x):
    lane = lax.broadcasted_iota(jnp.int32, x.shape, x.ndim - 1)
    same = (sublanes(x.shape) < 4) == (lane < 64)
    return jnp.where(same, x, jnp.roll(jnp.roll(x, 4, axis=x.ndim - 2), 64, axis=x.ndim - 1))


def right_kernel(rows_ref, left_ref, out_ref):
    place = lax.axis_index("col")
    last = rows_ref[0, 120:126, :]
    corner = straight(jnp.concatenate([last[0:2], jnp.zeros((2, 128), jnp.float32), last[2:6]], axis=0))
    total = None
    for q in range(16):
        if q == 0:
            x = jnp.concatenate([corner, jnp.zeros((120, 128), jnp.float32)], axis=0)
        else:
            x = straight(rows_ref[:, 8 * q - 8 : 8 * q, :]).reshape(128, 128)
        y = jnp.concatenate(
            [left_ref[0, 128 * q : 128 * q + 128, :], left_ref[1, 128 * q : 128 * q + 128, :]], axis=1
        )
        xh, xl = split(x)
        yh, yl = split(y * DOWN_PRODUCT)
        term = dot(xh, yh) + (dot(xh, yl) + dot(xl, yh))
        total = term if total is None else total + term
    by_real = total[:, :128].reshape(16, 8, 128)
    by_imag = jnp.roll(total[:, 128:].reshape(16, 8, 128), 4, axis=1)
    product = by_real + jnp.where(sublanes((16, 8, 128)) < 4, -by_imag, by_imag)
    start = pl.multiple_of(jnp.maximum(place - 1, 0) * 8, 8)
    block = straight(rows_ref[:, pl.ds(start, 8), :])
    which = lax.broadcasted_iota(jnp.int32, (16, 8, 128), 0)
    block = jnp.where(place == 0, jnp.where(which == 0, corner[None], 0.0), block)
    for n, x in enumerate((block * DOWN_INVERSE, product)):
        x = x.reshape(PAIRS, 2, 8, 128)
        real, imag = interleave(x[:, 0], x[:, 1])
        for d in range(16):
            out_ref[d, :, 2 * n] = real
            out_ref[d, :, 2 * n + 1] = imag


def tiles(block):
    first = sublanes((8, 8, 128)) < 4
    low, high = block[0:8], block[8:16]
    pair = (jnp.where(first, low, jnp.roll(high, 4, axis=1)), jnp.where(first, jnp.roll(low, 4, axis=1), high))
    return jnp.concatenate(pair, axis=0).reshape(128, 128)


def dot3(left_high, left_low, right):
    high, low = split(right)
    return dot(left_high, high) + (dot(left_high, low) + dot(left_low, high))


def first_kernel(rows_ref, right_ref, out_ref, later_ref, factor_ref, held_ref, sems):
    copies = [pltpu.make_async_copy(rows_ref.at[z], held_ref.at[z], sems.at[z]) for z in range(16)]
    for copy in copies:
        copy.start()
    core = lax.axis_index("c")
    shift = jnp.where(core == 0, 2, 126)
    keep = ((lax.broadcasted_iota(jnp.int32, (128, 128), 1) & 3) < 2) == (core == 0)
    total = None
    for step in range(PAIRS // DEPTH):
        lefts, rights = [], []
        for n in range(step * DEPTH, step * DEPTH + DEPTH):
            copies[2 * n].wait()
            copies[2 * n + 1].wait()
            blocks = []
            for p in range(2):
                for i in range(2):
                    at = slice(256 * i + 128 * p, 256 * i + 128 * p + 128)
                    near, far = held_ref[2 * n + core, at], held_ref[2 * n + 1 - core, at]
                    blocks.append(jnp.where(keep, near, pltpu.roll(far, shift, 1)))
                    high, low = split(jnp.where(keep, pltpu.roll(near, 128 - shift, 1), far))
                    span = slice(256 * p + 128 * i, 256 * p + 128 * i + 128)
                    later_ref[0, span, 128 * n : 128 * n + 128] = high
                    later_ref[1, span, 128 * n : 128 * n + 128] = low
            lefts.append(jnp.concatenate(blocks, axis=0))
            rights.append(jnp.concatenate([tiles(right_ref[:, n, m]) for m in range(4)], axis=1))
        high, low = split(jnp.concatenate(lefts, axis=1))
        term = dot3(high, low, jnp.concatenate(rights, axis=0))
        total = term if total is None else total + term
    out_ref[...] = total
    entries = jnp.sum(held_ref[:, ROWS : ROWS + 8], axis=0)
    for i in range(2):
        real, imag = entries[2 * i : 2 * i + 1], entries[2 * i + 1 : 2 * i + 2]
        magnitude = jnp.maximum(real * real + imag * imag, 1.0)
        factor_ref[2 * i : 2 * i + 1, :] = real / magnitude
        factor_ref[2 * i + 1 : 2 * i + 2, :] = -imag / magnitude
    factor_ref[4:8, :] = jnp.zeros((4, 128), jnp.float32)


def second_kernel(
    factor_ref, start_ref, left_ref, right_ref, panel_ref, cores_ref, near_ref, panel_vmem, cores_vmem, sems, out_sems
):
    copies = [
        [
            pltpu.make_async_copy(right_ref.at[:, z, 2 * n : 2 * n + 2], near_ref.at[n, z], sems.at[n, z])
            for z in range(PAIRS)
        ]
        for n in range(2)
    ]
    for copy in copies[0] + copies[1]:
        copy.start()
    columns = factor_ref[...].T
    results = (
        (pltpu.make_async_copy(panel_vmem, panel_ref, out_sems.at[0]), panel_vmem, UP_INVERSE),
        (pltpu.make_async_copy(cores_vmem, cores_ref, out_sems.at[1]), cores_vmem, UP_PRODUCT),
    )
    for n, (result, out, up) in enumerate(results):
        for copy in copies[n]:
            copy.wait()
        right = jnp.concatenate(
            [
                jnp.concatenate([tiles(near_ref[n, z, :, p]) for p in range(2)], axis=1)
                for z in range(PAIRS)
            ],
            axis=0,
        )
        total = start_ref[:, 256 * n : 256 * n + 256] + dot3(left_ref[0], left_ref[1], right)
        for i in range(2):
            fr, fi = columns[:, 2 * i : 2 * i + 1], columns[:, 2 * i + 1 : 2 * i + 2]
            by_real, by_imag = total[128 * i : 128 * i + 128], total[256 + 128 * i : 384 + 128 * i]
            real = by_real[:, :128] - by_imag[:, 128:]
            imag = by_real[:, 128:] + by_imag[:, :128]
            where = (i,) if n == 0 else (i, 0)
            out[where + (0,)] = (fr * real - fi * imag) * up
            out[where + (1,)] = (fr * imag + fi * real) * up
        result.start()
    for result, _, _ in results:
        result.wait()


def first_call(rows, right):
    vmem = pl.BlockSpec(memory_space=pltpu.VMEM)
    return pl.pallas_call(
        first_kernel,
        in_specs=[pl.BlockSpec(memory_space=pltpu.HBM), vmem],
        out_specs=(vmem, vmem, vmem),
        out_shape=(
            jax.ShapeDtypeStruct((512, 512), jnp.float32),
            jax.ShapeDtypeStruct((2, 512, 1024), jnp.bfloat16),
            jax.ShapeDtypeStruct((8, 128), jnp.float32),
        ),
        scratch_shapes=[pltpu.VMEM((16, ROWS + 8, 128), jnp.float32), pltpu.SemaphoreType.DMA((16,))],
        compiler_params=params(48),
        cost_estimate=cost(2 * 3 * 512 * 1024 * 512, 7 * 2**20),
    )(rows, right)


def second_call(factor, start, left, right):
    vmem = pl.BlockSpec(memory_space=pltpu.VMEM)
    hbm = pl.BlockSpec(memory_space=pltpu.HBM)
    shapes = (2, 2, 128, 128), (2, 1, 2, 128, 128)
    return pl.pallas_call(
        second_kernel,
        in_specs=[vmem, vmem, vmem, hbm],
        out_specs=(hbm, hbm),
        out_shape=tuple(jax.ShapeDtypeStruct(shape, jnp.float32) for shape in shapes),
        scratch_shapes=[
            pltpu.VMEM((2, PAIRS, 16, 2, 8, 128), jnp.float32),
            pltpu.VMEM(shapes[0], jnp.float32),
            pltpu.VMEM(shapes[1], jnp.float32),
            pltpu.SemaphoreType.DMA((2, PAIRS)),
            pltpu.SemaphoreType.DMA((2,)),
        ],
        compiler_params=params(48),
        cost_estimate=cost(2 * 3 * 512 * 1024 * 512, 8 * 2**20),
    )(factor, start, left, right)


def on_device(col_samples, row_samples, pivot_rows, rank_blocks, upper_inverse, upanel_left):
    f32 = jnp.float32
    vmem = pl.BlockSpec(memory_space=pltpu.VMEM)
    hbm = pl.BlockSpec(memory_space=pltpu.HBM)
    packed, sent = pl.pallas_call(
        start_kernel,
        in_specs=[hbm] * 5,
        out_specs=(vmem, hbm),
        out_shape=(jax.ShapeDtypeStruct((16, 8, 128), f32), jax.ShapeDtypeStruct((ROWS + 8, 128), f32)),
        scratch_shapes=[
            pltpu.VMEM((2, 64, 128), f32),
            pltpu.VMEM(col_samples.shape, f32),
            pltpu.VMEM(pivot_rows.shape, jnp.int32),
            pltpu.SMEM(rank_blocks.shape, jnp.int32),
            pltpu.VMEM((8, 128), f32),
            pltpu.SemaphoreType.DMA((6,)),
        ],
        compiler_params=params(61.75),
        cost_estimate=cost(2**17, 2**18),
    )(jnp.swapaxes(upper_inverse, 1, 2), row_samples.reshape(ROWS, 128), col_samples, pivot_rows, rank_blocks)
    rows = lax.all_gather(sent, "col", axis=0)
    packed = lax.all_to_all(packed.reshape(32, 4, 128), CHIPS + ("c",), 0, 0).reshape(128, 128)
    packed = jnp.concatenate([packed[8:], packed[0:2], packed[4:8]], axis=0)
    packed = lax.all_gather(packed, "col", axis=0)
    right = pl.pallas_call(
        right_kernel,
        in_specs=[vmem, vmem],
        out_specs=vmem,
        out_shape=jax.ShapeDtypeStruct((16, PAIRS, 4, 8, 128), f32),
        compiler_params=params(),
        cost_estimate=cost(2 * 3 * 128 * 2048 * 256, 5 * 2**20),
    )(packed, upanel_left[0])
    own = lax.all_to_all(right, CHIPS, 0, 0)
    other = lax.ppermute(own, "c", [(0, 1), (1, 0)])
    start, left, factor = first_call(rows, own)
    return second_call(factor, start, left, other)


def solution(mesh):
    chips = mesh.devices.reshape(4, 4, 2, 16)
    fine = Mesh(chips, ("y", "x", "c", "col"))
    row = ("y", "x", "c")
    in_specs = (
        P(row, None, "col", None),
        P(row, None, None, "col"),
        P(row, None),
        P(row),
        P(None, "col", row),
        P("col", None, None, None),
    )
    out_specs = (P(row, None, None, "col"), P(row, "col", None, None, None))
    return jax.shard_map(
        on_device, mesh=fine, in_specs=in_specs, out_specs=out_specs, check_vma=False
    )
```

```python
import jax
import jax.numpy as jnp
from jax import lax
from jax.experimental import pallas as pl
from jax.experimental.pallas import tpu as pltpu
from jax.sharding import Mesh
from jax.sharding import PartitionSpec as P

RANK_STEP = 16
CHIPS = ("y", "x")
DOWN_INVERSE, UP_INVERSE = 2.0 ** -16, 2.0 ** 16
DOWN_PRODUCT, UP_PRODUCT = 2.0 ** -24, 2.0 ** 24
PAIRS = 8
DEPTH = 4
ROWS = 512


def params(mebibytes=24):
    return pltpu.CompilerParams(vmem_limit_bytes=int(mebibytes * 2**20))


def cost(flops, moved):
    return pl.CostEstimate(flops=flops, bytes_accessed=moved, transcendentals=0)


def split(x):
    high = x.astype(jnp.bfloat16)
    low = (x - high.astype(jnp.float32)).astype(jnp.bfloat16)
    return high, low


def dot(a, b):
    return jnp.dot(a, b, preferred_element_type=jnp.float32)


def sublanes(shape):
    return lax.broadcasted_iota(jnp.int32, shape, len(shape) - 2)


def interleave(even, odd):
    row = sublanes(even.shape)

    def turn(x, n):
        return jnp.roll(x, n, axis=x.ndim - 2)

    even2, odd2, even4, odd4, even6, odd6 = (turn(x, n) for n in (2, 4, 6) for x in (even, odd))
    low = jnp.where(row < 2, even, jnp.where(row < 4, odd2, jnp.where(row < 6, even2, odd4)))
    high = jnp.where(row < 2, even4, jnp.where(row < 4, odd6, jnp.where(row < 6, even6, odd)))
    return low, high


def start_kernel(
    block_hbm, rows_hbm, cols_hbm, pivots_hbm, ranks_hbm, out_ref, sent_ref, block_ref, cols_ref, pivots_ref, ranks_ref, sems
):
    pairs = (
        (block_hbm, block_ref),
        (cols_hbm, cols_ref),
        (pivots_hbm, pivots_ref),
        (ranks_hbm, ranks_ref),
        (rows_hbm, sent_ref.at[0:ROWS]),
    )
    copies = [pltpu.make_async_copy(a, b, sems.at[n]) for n, (a, b) in enumerate(pairs)]
    for copy in copies:
        copy.start()
    copies[0].wait()
    rows = jnp.concatenate([block_ref[0].T, block_ref[1].T], axis=1).reshape(16, 8, 128)
    low, high = interleave(rows[:8], rows[8:])
    out_ref[0:8] = low
    out_ref[8:16] = high
    for copy in copies[1:4]:
        copy.wait()
    width = cols_ref.shape[2]
    levels = lax.broadcasted_iota(jnp.int32, (1, cols_ref.shape[3]), 1)
    rows = lax.broadcasted_iota(jnp.int32, cols_ref.shape[2:], 0) + lax.axis_index("col") * width
    for i in range(2):
        hit = jnp.logical_and(pivots_ref[i : i + 1, :] == rows, levels < RANK_STEP * ranks_ref[i])
        for p in range(2):
            at = ROWS + 2 * i + p
            sent_ref[at : at + 1, :] = jnp.sum(jnp.where(hit, cols_ref[i, p], 0.0), axis=0, keepdims=True)
    sent_ref[ROWS + 4 : ROWS + 8, :] = jnp.zeros((4, 128), jnp.float32)
    copies[4].wait()


def straight(x):
    lane = lax.broadcasted_iota(jnp.int32, x.shape, x.ndim - 1)
    same = (sublanes(x.shape) < 4) == (lane < 64)
    return jnp.where(same, x, jnp.roll(jnp.roll(x, 4, axis=x.ndim - 2), 64, axis=x.ndim - 1))


def right_kernel(rows_ref, left_ref, out_ref):
    place = lax.axis_index("col")
    last = rows_ref[0, 120:126, :]
    corner = straight(jnp.concatenate([last[0:2], jnp.zeros((2, 128), jnp.float32), last[2:6]], axis=0))
    total = None
    for q in range(16):
        if q == 0:
            x = jnp.concatenate([corner, jnp.zeros((120, 128), jnp.float32)], axis=0)
        else:
            x = straight(rows_ref[:, 8 * q - 8 : 8 * q, :]).reshape(128, 128)
        y = jnp.concatenate(
            [left_ref[0, 128 * q : 128 * q + 128, :], left_ref[1, 128 * q : 128 * q + 128, :]], axis=1
        )
        xh, xl = split(x)
        yh, yl = split(y * DOWN_PRODUCT)
        term = dot(xh, yh) + (dot(xh, yl) + dot(xl, yh))
        total = term if total is None else total + term
    by_real = total[:, :128].reshape(16, 8, 128)
    by_imag = jnp.roll(total[:, 128:].reshape(16, 8, 128), 4, axis=1)
    product = by_real + jnp.where(sublanes((16, 8, 128)) < 4, -by_imag, by_imag)
    start = pl.multiple_of(jnp.maximum(place - 1, 0) * 8, 8)
    block = straight(rows_ref[:, pl.ds(start, 8), :])
    which = lax.broadcasted_iota(jnp.int32, (16, 8, 128), 0)
    block = jnp.where(place == 0, jnp.where(which == 0, corner[None], 0.0), block)
    for n, x in enumerate((block * DOWN_INVERSE, product)):
        x = x.reshape(PAIRS, 2, 8, 128)
        real, imag = interleave(x[:, 0], x[:, 1])
        for d in range(16):
            out_ref[d, :, 2 * n] = real
            out_ref[d, :, 2 * n + 1] = imag


def tiles(block):
    first = sublanes((8, 8, 128)) < 4
    low, high = block[0:8], block[8:16]
    pair = (jnp.where(first, low, jnp.roll(high, 4, axis=1)), jnp.where(first, jnp.roll(low, 4, axis=1), high))
    return jnp.concatenate(pair, axis=0).reshape(128, 128)


def dot3(left_high, left_low, right):
    high, low = split(right)
    return dot(left_high, high) + (dot(left_high, low) + dot(left_low, high))


def first_kernel(rows_ref, right_ref, out_ref, later_ref, factor_ref, held_ref, sems):
    copies = [pltpu.make_async_copy(rows_ref.at[z], held_ref.at[z], sems.at[z]) for z in range(16)]
    for copy in copies:
        copy.start()
    core = lax.axis_index("c")
    shift = jnp.where(core == 0, 2, 126)
    keep = ((lax.broadcasted_iota(jnp.int32, (128, 128), 1) & 3) < 2) == (core == 0)
    total = None
    for step in range(PAIRS // DEPTH):
        lefts, rights = [], []
        for n in range(step * DEPTH, step * DEPTH + DEPTH):
            copies[2 * n].wait()
            copies[2 * n + 1].wait()
            blocks = []
            for p in range(2):
                for i in range(2):
                    at = slice(256 * i + 128 * p, 256 * i + 128 * p + 128)
                    near, far = held_ref[2 * n + core, at], held_ref[2 * n + 1 - core, at]
                    blocks.append(jnp.where(keep, near, pltpu.roll(far, shift, 1)))
                    high, low = split(jnp.where(keep, pltpu.roll(near, 128 - shift, 1), far))
                    span = slice(256 * p + 128 * i, 256 * p + 128 * i + 128)
                    later_ref[0, span, 128 * n : 128 * n + 128] = high
                    later_ref[1, span, 128 * n : 128 * n + 128] = low
            lefts.append(jnp.concatenate(blocks, axis=0))
            rights.append(jnp.concatenate([tiles(right_ref[:, n, m]) for m in range(4)], axis=1))
        high, low = split(jnp.concatenate(lefts, axis=1))
        term = dot3(high, low, jnp.concatenate(rights, axis=0))
        total = term if total is None else total + term
    out_ref[...] = total
    entries = jnp.sum(held_ref[:, ROWS : ROWS + 8], axis=0)
    for i in range(2):
        real, imag = entries[2 * i : 2 * i + 1], entries[2 * i + 1 : 2 * i + 2]
        magnitude = jnp.maximum(real * real + imag * imag, 1.0)
        factor_ref[2 * i : 2 * i + 1, :] = real / magnitude
        factor_ref[2 * i + 1 : 2 * i + 2, :] = -imag / magnitude
    factor_ref[4:8, :] = jnp.zeros((4, 128), jnp.float32)


def second_kernel(
    factor_ref, start_ref, left_ref, right_ref, panel_ref, cores_ref, near_ref, panel_vmem, cores_vmem, sems, out_sems
):
    copies = [
        [
            pltpu.make_async_copy(right_ref.at[:, z, 2 * n : 2 * n + 2], near_ref.at[n, z], sems.at[n, z])
            for z in range(PAIRS)
        ]
        for n in range(2)
    ]
    for copy in copies[0] + copies[1]:
        copy.start()
    columns = factor_ref[...].T
    results = (
        (pltpu.make_async_copy(panel_vmem, panel_ref, out_sems.at[0]), panel_vmem, UP_INVERSE),
        (pltpu.make_async_copy(cores_vmem, cores_ref, out_sems.at[1]), cores_vmem, UP_PRODUCT),
    )
    for n, (result, out, up) in enumerate(results):
        for copy in copies[n]:
            copy.wait()
        right = jnp.concatenate(
            [
                jnp.concatenate([tiles(near_ref[n, z, :, p]) for p in range(2)], axis=1)
                for z in range(PAIRS)
            ],
            axis=0,
        )
        total = start_ref[:, 256 * n : 256 * n + 256] + dot3(left_ref[0], left_ref[1], right)
        for i in range(2):
            fr, fi = columns[:, 2 * i : 2 * i + 1], columns[:, 2 * i + 1 : 2 * i + 2]
            by_real, by_imag = total[128 * i : 128 * i + 128], total[256 + 128 * i : 384 + 128 * i]
            real = by_real[:, :128] - by_imag[:, 128:]
            imag = by_real[:, 128:] + by_imag[:, :128]
            where = (i,) if n == 0 else (i, 0)
            out[where + (0,)] = (fr * real - fi * imag) * up
            out[where + (1,)] = (fr * imag + fi * real) * up
        result.start()
    for result, _, _ in results:
        result.wait()


def first_call(rows, right):
    vmem = pl.BlockSpec(memory_space=pltpu.VMEM)
    return pl.pallas_call(
        first_kernel,
        in_specs=[pl.BlockSpec(memory_space=pltpu.HBM), vmem],
        out_specs=(vmem, vmem, vmem),
        out_shape=(
            jax.ShapeDtypeStruct((512, 512), jnp.float32),
            jax.ShapeDtypeStruct((2, 512, 1024), jnp.bfloat16),
            jax.ShapeDtypeStruct((8, 128), jnp.float32),
        ),
        scratch_shapes=[pltpu.VMEM((16, ROWS + 8, 128), jnp.float32), pltpu.SemaphoreType.DMA((16,))],
        compiler_params=params(48),
        cost_estimate=cost(2 * 3 * 512 * 1024 * 512, 7 * 2**20),
    )(rows, right)


def second_call(factor, start, left, right):
    vmem = pl.BlockSpec(memory_space=pltpu.VMEM)
    hbm = pl.BlockSpec(memory_space=pltpu.HBM)
    shapes = (2, 2, 128, 128), (2, 1, 2, 128, 128)
    return pl.pallas_call(
        second_kernel,
        in_specs=[vmem, vmem, vmem, hbm],
        out_specs=(hbm, hbm),
        out_shape=tuple(jax.ShapeDtypeStruct(shape, jnp.float32) for shape in shapes),
        scratch_shapes=[
            pltpu.VMEM((2, PAIRS, 16, 2, 8, 128), jnp.float32),
            pltpu.VMEM(shapes[0], jnp.float32),
            pltpu.VMEM(shapes[1], jnp.float32),
            pltpu.SemaphoreType.DMA((2, PAIRS)),
            pltpu.SemaphoreType.DMA((2,)),
        ],
        compiler_params=params(48),
        cost_estimate=cost(2 * 3 * 512 * 1024 * 512, 8 * 2**20),
    )(factor, start, left, right)


def on_device(col_samples, row_samples, pivot_rows, rank_blocks, upper_inverse, upanel_left):
    f32 = jnp.float32
    vmem = pl.BlockSpec(memory_space=pltpu.VMEM)
    hbm = pl.BlockSpec(memory_space=pltpu.HBM)
    packed, sent = pl.pallas_call(
        start_kernel,
        in_specs=[hbm] * 5,
        out_specs=(vmem, vmem),
        out_shape=(jax.ShapeDtypeStruct((16, 8, 128), f32), jax.ShapeDtypeStruct((ROWS + 8, 128), f32)),
        scratch_shapes=[
            pltpu.VMEM((2, 64, 128), f32),
            pltpu.VMEM(col_samples.shape, f32),
            pltpu.VMEM(pivot_rows.shape, jnp.int32),
            pltpu.SMEM(rank_blocks.shape, jnp.int32),
            pltpu.SemaphoreType.DMA((5,)),
        ],
        compiler_params=params(61.75),
        cost_estimate=cost(2**17, 2**18),
    )(jnp.swapaxes(upper_inverse, 1, 2), row_samples.reshape(ROWS, 128), col_samples, pivot_rows, rank_blocks)
    rows = lax.all_gather(sent, "col", axis=0)
    packed = lax.all_to_all(packed.reshape(32, 4, 128), CHIPS + ("c",), 0, 0).reshape(128, 128)
    packed = jnp.concatenate([packed[8:], packed[0:2], packed[4:8]], axis=0)
    packed = lax.all_gather(packed, "col", axis=0)
    right = pl.pallas_call(
        right_kernel,
        in_specs=[vmem, vmem],
        out_specs=vmem,
        out_shape=jax.ShapeDtypeStruct((16, PAIRS, 4, 8, 128), f32),
        compiler_params=params(),
        cost_estimate=cost(2 * 3 * 128 * 2048 * 256, 5 * 2**20),
    )(packed, upanel_left[0])
    own = lax.all_to_all(right, CHIPS, 0, 0)
    other = lax.ppermute(own, "c", [(0, 1), (1, 0)])
    start, left, factor = first_call(rows, own)
    return second_call(factor, start, left, other)


def solution(mesh):
    chips = mesh.devices.reshape(4, 4, 2, 16)
    fine = Mesh(chips, ("y", "x", "c", "col"))
    row = ("y", "x", "c")
    in_specs = (
        P(row, None, "col", None),
        P(row, None, None, "col"),
        P(row, None),
        P(row),
        P(None, "col", row),
        P("col", None, None, None),
    )
    out_specs = (P(row, None, None, "col"), P(row, "col", None, None, None))
    return jax.shard_map(
        on_device, mesh=fine, in_specs=in_specs, out_specs=out_specs, check_vma=False
    )
```

```python
import jax
import jax.numpy as jnp
from jax import lax
from jax.experimental import pallas as pl
from jax.experimental.pallas import tpu as pltpu
from jax.sharding import Mesh
from jax.sharding import PartitionSpec as P

RANK_STEP = 16
CHIPS = ("y", "x")
DOWN_INVERSE, UP_INVERSE = 2.0 ** -16, 2.0 ** 16
DOWN_PRODUCT, UP_PRODUCT = 2.0 ** -24, 2.0 ** 24
PAIRS = 8
DEPTH = 2
ROWS = 512


def params(mebibytes=24):
    return pltpu.CompilerParams(vmem_limit_bytes=int(mebibytes * 2**20))


def cost(flops, moved):
    return pl.CostEstimate(flops=flops, bytes_accessed=moved, transcendentals=0)


def split(x):
    high = x.astype(jnp.bfloat16)
    low = (x - high.astype(jnp.float32)).astype(jnp.bfloat16)
    return high, low


def dot(a, b):
    return jnp.dot(a, b, preferred_element_type=jnp.float32)


def sublanes(shape):
    return lax.broadcasted_iota(jnp.int32, shape, len(shape) - 2)


def interleave(even, odd):
    row = sublanes(even.shape)

    def turn(x, n):
        return jnp.roll(x, n, axis=x.ndim - 2)

    even2, odd2, even4, odd4, even6, odd6 = (turn(x, n) for n in (2, 4, 6) for x in (even, odd))
    low = jnp.where(row < 2, even, jnp.where(row < 4, odd2, jnp.where(row < 6, even2, odd4)))
    high = jnp.where(row < 2, even4, jnp.where(row < 4, odd6, jnp.where(row < 6, even6, odd)))
    return low, high


def start_kernel(
    block_hbm, rows_hbm, cols_hbm, pivots_hbm, ranks_hbm, out_ref, sent_ref, block_ref, cols_ref, pivots_ref, ranks_ref, sems
):
    pairs = (
        (block_hbm, block_ref),
        (cols_hbm, cols_ref),
        (pivots_hbm, pivots_ref),
        (ranks_hbm, ranks_ref),
        (rows_hbm, sent_ref.at[0:ROWS]),
    )
    copies = [pltpu.make_async_copy(a, b, sems.at[n]) for n, (a, b) in enumerate(pairs)]
    for copy in copies:
        copy.start()
    copies[0].wait()
    rows = jnp.concatenate([block_ref[0].T, block_ref[1].T], axis=1).reshape(16, 8, 128)
    low, high = interleave(rows[:8], rows[8:])
    out_ref[0:8] = low
    out_ref[8:16] = high
    for copy in copies[1:4]:
        copy.wait()
    width = cols_ref.shape[2]
    levels = lax.broadcasted_iota(jnp.int32, (1, cols_ref.shape[3]), 1)
    rows = lax.broadcasted_iota(jnp.int32, cols_ref.shape[2:], 0) + lax.axis_index("col") * width
    for i in range(2):
        hit = jnp.logical_and(pivots_ref[i : i + 1, :] == rows, levels < RANK_STEP * ranks_ref[i])
        for p in range(2):
            at = ROWS + 2 * i + p
            sent_ref[at : at + 1, :] = jnp.sum(jnp.where(hit, cols_ref[i, p], 0.0), axis=0, keepdims=True)
    sent_ref[ROWS + 4 : ROWS + 8, :] = jnp.zeros((4, 128), jnp.float32)
    copies[4].wait()


def straight(x):
    lane = lax.broadcasted_iota(jnp.int32, x.shape, x.ndim - 1)
    same = (sublanes(x.shape) < 4) == (lane < 64)
    return jnp.where(same, x, jnp.roll(jnp.roll(x, 4, axis=x.ndim - 2), 64, axis=x.ndim - 1))


def right_kernel(rows_ref, left_ref, out_ref):
    place = lax.axis_index("col")
    last = rows_ref[0, 120:126, :]
    corner = straight(jnp.concatenate([last[0:2], jnp.zeros((2, 128), jnp.float32), last[2:6]], axis=0))
    total = None
    for q in range(16):
        if q == 0:
            x = jnp.concatenate([corner, jnp.zeros((120, 128), jnp.float32)], axis=0)
        else:
            x = straight(rows_ref[:, 8 * q - 8 : 8 * q, :]).reshape(128, 128)
        y = jnp.concatenate(
            [left_ref[0, 128 * q : 128 * q + 128, :], left_ref[1, 128 * q : 128 * q + 128, :]], axis=1
        )
        xh, xl = split(x)
        yh, yl = split(y * DOWN_PRODUCT)
        term = dot(xh, yh) + (dot(xh, yl) + dot(xl, yh))
        total = term if total is None else total + term
    by_real = total[:, :128].reshape(16, 8, 128)
    by_imag = jnp.roll(total[:, 128:].reshape(16, 8, 128), 4, axis=1)
    product = by_real + jnp.where(sublanes((16, 8, 128)) < 4, -by_imag, by_imag)
    start = pl.multiple_of(jnp.maximum(place - 1, 0) * 8, 8)
    block = straight(rows_ref[:, pl.ds(start, 8), :])
    which = lax.broadcasted_iota(jnp.int32, (16, 8, 128), 0)
    block = jnp.where(place == 0, jnp.where(which == 0, corner[None], 0.0), block)
    for n, x in enumerate((block * DOWN_INVERSE, product)):
        x = x.reshape(PAIRS, 2, 8, 128)
        real, imag = interleave(x[:, 0], x[:, 1])
        for d in range(16):
            out_ref[d, :, 2 * n] = real
            out_ref[d, :, 2 * n + 1] = imag


def tiles(block):
    first = sublanes((8, 8, 128)) < 4
    low, high = block[0:8], block[8:16]
    pair = (jnp.where(first, low, jnp.roll(high, 4, axis=1)), jnp.where(first, jnp.roll(low, 4, axis=1), high))
    return jnp.concatenate(pair, axis=0).reshape(128, 128)


def dot3(left, right):
    return dot(left[0], right[0]) + (dot(left[0], right[1]) + dot(left[1], right[0]))


def first_kernel(rows_ref, right_ref, out_ref, later_ref, factor_ref, held_ref, high_ref, low_ref, sems):
    copies = [pltpu.make_async_copy(rows_ref.at[z], held_ref.at[z], sems.at[z]) for z in range(16)]
    for copy in copies:
        copy.start()
    core = lax.axis_index("c")
    shift = jnp.where(core == 0, 2, 126)
    keep = ((lax.broadcasted_iota(jnp.int32, (128, 128), 1) & 3) < 2) == (core == 0)
    for n in range(PAIRS):
        right = jnp.concatenate([tiles(right_ref[:, n, m]) for m in range(4)], axis=1)
        high_ref[128 * n : 128 * n + 128, :], low_ref[128 * n : 128 * n + 128, :] = split(right)
    total = None
    for step in range(PAIRS // DEPTH):
        lefts = []
        for n in range(step * DEPTH, step * DEPTH + DEPTH):
            copies[2 * n].wait()
            copies[2 * n + 1].wait()
            blocks = []
            for p in range(2):
                for i in range(2):
                    at = slice(256 * i + 128 * p, 256 * i + 128 * p + 128)
                    near, far = held_ref[2 * n + core, at], held_ref[2 * n + 1 - core, at]
                    blocks.append(jnp.where(keep, near, pltpu.roll(far, shift, 1)))
                    high, low = split(jnp.where(keep, pltpu.roll(near, 128 - shift, 1), far))
                    span = slice(256 * p + 128 * i, 256 * p + 128 * i + 128)
                    later_ref[0, span, 128 * n : 128 * n + 128] = high
                    later_ref[1, span, 128 * n : 128 * n + 128] = low
            lefts.append(jnp.concatenate(blocks, axis=0))
        at = slice(128 * DEPTH * step, 128 * DEPTH * step + 128 * DEPTH)
        term = dot3(split(jnp.concatenate(lefts, axis=1)), (high_ref[at, :], low_ref[at, :]))
        total = term if total is None else total + term
    out_ref[...] = total
    entries = jnp.sum(held_ref[:, ROWS : ROWS + 8], axis=0)
    for i in range(2):
        real, imag = entries[2 * i : 2 * i + 1], entries[2 * i + 1 : 2 * i + 2]
        magnitude = jnp.maximum(real * real + imag * imag, 1.0)
        factor_ref[2 * i : 2 * i + 1, :] = real / magnitude
        factor_ref[2 * i + 1 : 2 * i + 2, :] = -imag / magnitude
    factor_ref[4:8, :] = jnp.zeros((4, 128), jnp.float32)


def second_kernel(
    factor_ref,
    start_ref,
    left_ref,
    right_ref,
    panel_ref,
    cores_ref,
    near_ref,
    high_ref,
    low_ref,
    panel_vmem,
    cores_vmem,
    sems,
    out_sems,
):
    copies = [
        [
            pltpu.make_async_copy(right_ref.at[:, z, 2 * n : 2 * n + 2], near_ref.at[n, z], sems.at[n, z])
            for z in range(PAIRS)
        ]
        for n in range(2)
    ]
    for copy in copies[0] + copies[1]:
        copy.start()
    columns = factor_ref[...].T
    results = (
        (pltpu.make_async_copy(panel_vmem, panel_ref, out_sems.at[0]), panel_vmem, UP_INVERSE),
        (pltpu.make_async_copy(cores_vmem, cores_ref, out_sems.at[1]), cores_vmem, UP_PRODUCT),
    )
    def ready(n):
        for z in range(PAIRS):
            copies[n][z].wait()
            right = jnp.concatenate([tiles(near_ref[n, z, :, p]) for p in range(2)], axis=1)
            high_ref[n, 128 * z : 128 * z + 128, :], low_ref[n, 128 * z : 128 * z + 128, :] = split(right)

    ready(0)
    ready(1)
    for n, (result, out, up) in enumerate(results):
        total = start_ref[:, 256 * n : 256 * n + 256] + dot3(left_ref, (high_ref[n], low_ref[n]))
        for i in range(2):
            fr, fi = columns[:, 2 * i : 2 * i + 1], columns[:, 2 * i + 1 : 2 * i + 2]
            by_real, by_imag = total[128 * i : 128 * i + 128], total[256 + 128 * i : 384 + 128 * i]
            real = by_real[:, :128] - by_imag[:, 128:]
            imag = by_real[:, 128:] + by_imag[:, :128]
            where = (i,) if n == 0 else (i, 0)
            out[where + (0,)] = (fr * real - fi * imag) * up
            out[where + (1,)] = (fr * imag + fi * real) * up
        result.start()
    for result, _, _ in results:
        result.wait()


def first_call(rows, right):
    vmem = pl.BlockSpec(memory_space=pltpu.VMEM)
    return pl.pallas_call(
        first_kernel,
        in_specs=[pl.BlockSpec(memory_space=pltpu.HBM), vmem],
        out_specs=(vmem, vmem, vmem),
        out_shape=(
            jax.ShapeDtypeStruct((512, 512), jnp.float32),
            jax.ShapeDtypeStruct((2, 512, 1024), jnp.bfloat16),
            jax.ShapeDtypeStruct((8, 128), jnp.float32),
        ),
        scratch_shapes=[
            pltpu.VMEM((16, ROWS + 8, 128), jnp.float32),
            pltpu.VMEM((1024, 512), jnp.bfloat16),
            pltpu.VMEM((1024, 512), jnp.bfloat16),
            pltpu.SemaphoreType.DMA((16,)),
        ],
        compiler_params=params(48),
        cost_estimate=cost(2 * 3 * 512 * 1024 * 512, 7 * 2**20),
    )(rows, right)


def second_call(factor, start, left, right):
    vmem = pl.BlockSpec(memory_space=pltpu.VMEM)
    hbm = pl.BlockSpec(memory_space=pltpu.HBM)
    shapes = (2, 2, 128, 128), (2, 1, 2, 128, 128)
    return pl.pallas_call(
        second_kernel,
        in_specs=[vmem, vmem, vmem, hbm],
        out_specs=(hbm, hbm),
        out_shape=tuple(jax.ShapeDtypeStruct(shape, jnp.float32) for shape in shapes),
        scratch_shapes=[
            pltpu.VMEM((2, PAIRS, 16, 2, 8, 128), jnp.float32),
            pltpu.VMEM((2, 1024, 256), jnp.bfloat16),
            pltpu.VMEM((2, 1024, 256), jnp.bfloat16),
            pltpu.VMEM(shapes[0], jnp.float32),
            pltpu.VMEM(shapes[1], jnp.float32),
            pltpu.SemaphoreType.DMA((2, PAIRS)),
            pltpu.SemaphoreType.DMA((2,)),
        ],
        compiler_params=params(48),
        cost_estimate=cost(2 * 3 * 512 * 1024 * 512, 8 * 2**20),
    )(factor, start, left, right)


def on_device(col_samples, row_samples, pivot_rows, rank_blocks, upper_inverse, upanel_left):
    f32 = jnp.float32
    vmem = pl.BlockSpec(memory_space=pltpu.VMEM)
    hbm = pl.BlockSpec(memory_space=pltpu.HBM)
    packed, sent = pl.pallas_call(
        start_kernel,
        in_specs=[hbm] * 5,
        out_specs=(vmem, vmem),
        out_shape=(jax.ShapeDtypeStruct((16, 8, 128), f32), jax.ShapeDtypeStruct((ROWS + 8, 128), f32)),
        scratch_shapes=[
            pltpu.VMEM((2, 64, 128), f32),
            pltpu.VMEM(col_samples.shape, f32),
            pltpu.VMEM(pivot_rows.shape, jnp.int32),
            pltpu.SMEM(rank_blocks.shape, jnp.int32),
            pltpu.SemaphoreType.DMA((5,)),
        ],
        compiler_params=params(61.75),
        cost_estimate=cost(2**17, 2**18),
    )(jnp.swapaxes(upper_inverse, 1, 2), row_samples.reshape(ROWS, 128), col_samples, pivot_rows, rank_blocks)
    rows = lax.all_gather(sent, "col", axis=0)
    packed = lax.all_to_all(packed.reshape(32, 4, 128), CHIPS + ("c",), 0, 0).reshape(128, 128)
    packed = jnp.concatenate([packed[8:], packed[0:2], packed[4:8]], axis=0)
    packed = lax.all_gather(packed, "col", axis=0)
    right = pl.pallas_call(
        right_kernel,
        in_specs=[vmem, vmem],
        out_specs=vmem,
        out_shape=jax.ShapeDtypeStruct((16, PAIRS, 4, 8, 128), f32),
        compiler_params=params(),
        cost_estimate=cost(2 * 3 * 128 * 2048 * 256, 5 * 2**20),
    )(packed, upanel_left[0])
    own = lax.all_to_all(right, CHIPS, 0, 0)
    other = lax.ppermute(own, "c", [(0, 1), (1, 0)])
    start, left, factor = first_call(rows, own)
    return second_call(factor, start, left, other)


def solution(mesh):
    chips = mesh.devices.reshape(4, 4, 2, 16)
    fine = Mesh(chips, ("y", "x", "c", "col"))
    row = ("y", "x", "c")
    in_specs = (
        P(row, None, "col", None),
        P(row, None, None, "col"),
        P(row, None),
        P(row),
        P(None, "col", row),
        P("col", None, None, None),
    )
    out_specs = (P(row, None, None, "col"), P(row, "col", None, None, None))
    return jax.shard_map(
        on_device, mesh=fine, in_specs=in_specs, out_specs=out_specs, check_vma=False
    )
```

```python
import jax
import jax.numpy as jnp
from jax import lax
from jax.experimental import pallas as pl
from jax.experimental.pallas import tpu as pltpu
from jax.sharding import Mesh
from jax.sharding import PartitionSpec as P

RANK_STEP = 16
CHIPS = ("y", "x")
DOWN_INVERSE, UP_INVERSE = 2.0 ** -16, 2.0 ** 16
DOWN_PRODUCT, UP_PRODUCT = 2.0 ** -24, 2.0 ** 24
PAIRS = 8
DEPTH = 2
ROWS = 512


def params(mebibytes=24):
    return pltpu.CompilerParams(vmem_limit_bytes=int(mebibytes * 2**20))


def cost(flops, moved):
    return pl.CostEstimate(flops=flops, bytes_accessed=moved, transcendentals=0)


def split(x):
    high = x.astype(jnp.bfloat16)
    low = (x - high.astype(jnp.float32)).astype(jnp.bfloat16)
    return high, low


def dot(a, b):
    return jnp.dot(a, b, preferred_element_type=jnp.float32)


def sublanes(shape):
    return lax.broadcasted_iota(jnp.int32, shape, len(shape) - 2)


def interleave(even, odd):
    row = sublanes(even.shape)

    def turn(x, n):
        return jnp.roll(x, n, axis=x.ndim - 2)

    even2, odd2, even4, odd4, even6, odd6 = (turn(x, n) for n in (2, 4, 6) for x in (even, odd))
    low = jnp.where(row < 2, even, jnp.where(row < 4, odd2, jnp.where(row < 6, even2, odd4)))
    high = jnp.where(row < 2, even4, jnp.where(row < 4, odd6, jnp.where(row < 6, even6, odd)))
    return low, high


def start_kernel(
    block_hbm, rows_hbm, cols_hbm, pivots_hbm, ranks_hbm, out_hbm, sent_hbm, block_ref, cols_ref, pivots_ref, ranks_ref, out_ref, sent_ref, sems
):
    pairs = (
        (block_hbm, block_ref),
        (cols_hbm, cols_ref),
        (pivots_hbm, pivots_ref),
        (ranks_hbm, ranks_ref),
        (rows_hbm, sent_ref.at[0:ROWS]),
    )
    copies = [pltpu.make_async_copy(a, b, sems.at[n]) for n, (a, b) in enumerate(pairs)]
    for copy in copies:
        copy.start()
    copies[0].wait()
    rows = jnp.concatenate([block_ref[0].T, block_ref[1].T], axis=1).reshape(16, 8, 128)
    low, high = interleave(rows[:8], rows[8:])
    out_ref[0:8] = low
    out_ref[8:16] = high
    results = [
        pltpu.make_async_copy(out_ref, out_hbm, sems.at[5]),
        pltpu.make_async_copy(sent_ref.at[0:ROWS], sent_hbm.at[0:ROWS], sems.at[6]),
        pltpu.make_async_copy(sent_ref.at[ROWS : ROWS + 8], sent_hbm.at[ROWS : ROWS + 8], sems.at[7]),
    ]
    results[0].start()
    copies[4].wait()
    results[1].start()
    for copy in copies[1:4]:
        copy.wait()
    width = cols_ref.shape[2]
    levels = lax.broadcasted_iota(jnp.int32, (1, cols_ref.shape[3]), 1)
    rows = lax.broadcasted_iota(jnp.int32, cols_ref.shape[2:], 0) + lax.axis_index("col") * width
    for i in range(2):
        hit = jnp.logical_and(pivots_ref[i : i + 1, :] == rows, levels < RANK_STEP * ranks_ref[i])
        for p in range(2):
            at = ROWS + 2 * i + p
            sent_ref[at : at + 1, :] = jnp.sum(jnp.where(hit, cols_ref[i, p], 0.0), axis=0, keepdims=True)
    sent_ref[ROWS + 4 : ROWS + 8, :] = jnp.zeros((4, 128), jnp.float32)
    results[2].start()
    for result in results:
        result.wait()


def straight(x):
    lane = lax.broadcasted_iota(jnp.int32, x.shape, x.ndim - 1)
    same = (sublanes(x.shape) < 4) == (lane < 64)
    return jnp.where(same, x, jnp.roll(jnp.roll(x, 4, axis=x.ndim - 2), 64, axis=x.ndim - 1))


def right_kernel(rows_ref, left_ref, out_ref):
    place = lax.axis_index("col")
    last = rows_ref[0, 120:126, :]
    corner = straight(jnp.concatenate([last[0:2], jnp.zeros((2, 128), jnp.float32), last[2:6]], axis=0))
    total = None
    for q in range(16):
        if q == 0:
            x = jnp.concatenate([corner, jnp.zeros((120, 128), jnp.float32)], axis=0)
        else:
            x = straight(rows_ref[:, 8 * q - 8 : 8 * q, :]).reshape(128, 128)
        y = jnp.concatenate(
            [left_ref[0, 128 * q : 128 * q + 128, :], left_ref[1, 128 * q : 128 * q + 128, :]], axis=1
        )
        xh, xl = split(x)
        yh, yl = split(y * DOWN_PRODUCT)
        term = dot(xh, yh) + (dot(xh, yl) + dot(xl, yh))
        total = term if total is None else total + term
    by_real = total[:, :128].reshape(16, 8, 128)
    by_imag = jnp.roll(total[:, 128:].reshape(16, 8, 128), 4, axis=1)
    product = by_real + jnp.where(sublanes((16, 8, 128)) < 4, -by_imag, by_imag)
    start = pl.multiple_of(jnp.maximum(place - 1, 0) * 8, 8)
    block = straight(rows_ref[:, pl.ds(start, 8), :])
    which = lax.broadcasted_iota(jnp.int32, (16, 8, 128), 0)
    block = jnp.where(place == 0, jnp.where(which == 0, corner[None], 0.0), block)
    for n, x in enumerate((block * DOWN_INVERSE, product)):
        x = x.reshape(PAIRS, 2, 8, 128)
        real, imag = interleave(x[:, 0], x[:, 1])
        for d in range(16):
            out_ref[d, :, 2 * n] = real
            out_ref[d, :, 2 * n + 1] = imag


def tiles(block):
    first = sublanes((8, 8, 128)) < 4
    low, high = block[0:8], block[8:16]
    pair = (jnp.where(first, low, jnp.roll(high, 4, axis=1)), jnp.where(first, jnp.roll(low, 4, axis=1), high))
    return jnp.concatenate(pair, axis=0).reshape(128, 128)


def dot3(left, right):
    return dot(left[0], right[0]) + (dot(left[0], right[1]) + dot(left[1], right[0]))


def first_kernel(rows_ref, right_ref, out_ref, later_ref, factor_ref, held_ref, high_ref, low_ref, sems):
    copies = [pltpu.make_async_copy(rows_ref.at[z], held_ref.at[z], sems.at[z]) for z in range(16)]
    for copy in copies:
        copy.start()
    core = lax.axis_index("c")
    shift = jnp.where(core == 0, 2, 126)
    keep = ((lax.broadcasted_iota(jnp.int32, (128, 128), 1) & 3) < 2) == (core == 0)
    for n in range(PAIRS):
        right = jnp.concatenate([tiles(right_ref[:, n, m]) for m in range(4)], axis=1)
        high_ref[128 * n : 128 * n + 128, :], low_ref[128 * n : 128 * n + 128, :] = split(right)
    total = None
    for step in range(PAIRS // DEPTH):
        lefts = []
        for n in range(step * DEPTH, step * DEPTH + DEPTH):
            copies[2 * n].wait()
            copies[2 * n + 1].wait()
            blocks = []
            for p in range(2):
                for i in range(2):
                    at = slice(256 * i + 128 * p, 256 * i + 128 * p + 128)
                    near, far = held_ref[2 * n + core, at], held_ref[2 * n + 1 - core, at]
                    blocks.append(jnp.where(keep, near, pltpu.roll(far, shift, 1)))
                    high, low = split(jnp.where(keep, pltpu.roll(near, 128 - shift, 1), far))
                    span = slice(256 * p + 128 * i, 256 * p + 128 * i + 128)
                    later_ref[0, span, 128 * n : 128 * n + 128] = high
                    later_ref[1, span, 128 * n : 128 * n + 128] = low
            lefts.append(jnp.concatenate(blocks, axis=0))
        at = slice(128 * DEPTH * step, 128 * DEPTH * step + 128 * DEPTH)
        term = dot3(split(jnp.concatenate(lefts, axis=1)), (high_ref[at, :], low_ref[at, :]))
        total = term if total is None else total + term
    out_ref[...] = total
    entries = jnp.sum(held_ref[:, ROWS : ROWS + 8], axis=0)
    for i in range(2):
        real, imag = entries[2 * i : 2 * i + 1], entries[2 * i + 1 : 2 * i + 2]
        magnitude = jnp.maximum(real * real + imag * imag, 1.0)
        factor_ref[2 * i : 2 * i + 1, :] = real / magnitude
        factor_ref[2 * i + 1 : 2 * i + 2, :] = -imag / magnitude
    factor_ref[4:8, :] = jnp.zeros((4, 128), jnp.float32)


def second_kernel(
    factor_ref,
    start_ref,
    left_ref,
    right_ref,
    panel_ref,
    cores_ref,
    near_ref,
    high_ref,
    low_ref,
    panel_vmem,
    cores_vmem,
    sems,
    out_sems,
):
    copies = [
        [
            pltpu.make_async_copy(right_ref.at[:, z, 2 * n : 2 * n + 2], near_ref.at[n, z], sems.at[n, z])
            for z in range(PAIRS)
        ]
        for n in range(2)
    ]
    for copy in copies[0] + copies[1]:
        copy.start()
    columns = factor_ref[...].T
    results = (
        (pltpu.make_async_copy(panel_vmem, panel_ref, out_sems.at[0]), panel_vmem, UP_INVERSE),
        (pltpu.make_async_copy(cores_vmem, cores_ref, out_sems.at[1]), cores_vmem, UP_PRODUCT),
    )
    def ready(n):
        for z in range(PAIRS):
            copies[n][z].wait()
            right = jnp.concatenate([tiles(near_ref[n, z, :, p]) for p in range(2)], axis=1)
            high_ref[n, 128 * z : 128 * z + 128, :], low_ref[n, 128 * z : 128 * z + 128, :] = split(right)

    ready(0)
    ready(1)
    for n, (result, out, up) in enumerate(results):
        total = start_ref[:, 256 * n : 256 * n + 256] + dot3(left_ref, (high_ref[n], low_ref[n]))
        for i in range(2):
            fr, fi = columns[:, 2 * i : 2 * i + 1], columns[:, 2 * i + 1 : 2 * i + 2]
            by_real, by_imag = total[128 * i : 128 * i + 128], total[256 + 128 * i : 384 + 128 * i]
            real = by_real[:, :128] - by_imag[:, 128:]
            imag = by_real[:, 128:] + by_imag[:, :128]
            where = (i,) if n == 0 else (i, 0)
            out[where + (0,)] = (fr * real - fi * imag) * up
            out[where + (1,)] = (fr * imag + fi * real) * up
        result.start()
    for result, _, _ in results:
        result.wait()


def first_call(rows, right):
    vmem = pl.BlockSpec(memory_space=pltpu.VMEM)
    return pl.pallas_call(
        first_kernel,
        in_specs=[pl.BlockSpec(memory_space=pltpu.HBM), vmem],
        out_specs=(vmem, vmem, vmem),
        out_shape=(
            jax.ShapeDtypeStruct((512, 512), jnp.float32),
            jax.ShapeDtypeStruct((2, 512, 1024), jnp.bfloat16),
            jax.ShapeDtypeStruct((8, 128), jnp.float32),
        ),
        scratch_shapes=[
            pltpu.VMEM((16, ROWS + 8, 128), jnp.float32),
            pltpu.VMEM((1024, 512), jnp.bfloat16),
            pltpu.VMEM((1024, 512), jnp.bfloat16),
            pltpu.SemaphoreType.DMA((16,)),
        ],
        compiler_params=params(48),
        cost_estimate=cost(2 * 3 * 512 * 1024 * 512, 7 * 2**20),
    )(rows, right)


def second_call(factor, start, left, right):
    vmem = pl.BlockSpec(memory_space=pltpu.VMEM)
    hbm = pl.BlockSpec(memory_space=pltpu.HBM)
    shapes = (2, 2, 128, 128), (2, 1, 2, 128, 128)
    return pl.pallas_call(
        second_kernel,
        in_specs=[vmem, vmem, vmem, hbm],
        out_specs=(hbm, hbm),
        out_shape=tuple(jax.ShapeDtypeStruct(shape, jnp.float32) for shape in shapes),
        scratch_shapes=[
            pltpu.VMEM((2, PAIRS, 16, 2, 8, 128), jnp.float32),
            pltpu.VMEM((2, 1024, 256), jnp.bfloat16),
            pltpu.VMEM((2, 1024, 256), jnp.bfloat16),
            pltpu.VMEM(shapes[0], jnp.float32),
            pltpu.VMEM(shapes[1], jnp.float32),
            pltpu.SemaphoreType.DMA((2, PAIRS)),
            pltpu.SemaphoreType.DMA((2,)),
        ],
        compiler_params=params(48),
        cost_estimate=cost(2 * 3 * 512 * 1024 * 512, 8 * 2**20),
    )(factor, start, left, right)


def on_device(col_samples, row_samples, pivot_rows, rank_blocks, upper_inverse, upanel_left):
    f32 = jnp.float32
    vmem = pl.BlockSpec(memory_space=pltpu.VMEM)
    hbm = pl.BlockSpec(memory_space=pltpu.HBM)
    packed, sent = pl.pallas_call(
        start_kernel,
        in_specs=[hbm] * 5,
        out_specs=(hbm, hbm),
        out_shape=(jax.ShapeDtypeStruct((16, 8, 128), f32), jax.ShapeDtypeStruct((ROWS + 8, 128), f32)),
        scratch_shapes=[
            pltpu.VMEM((2, 64, 128), f32),
            pltpu.VMEM(col_samples.shape, f32),
            pltpu.VMEM(pivot_rows.shape, jnp.int32),
            pltpu.SMEM(rank_blocks.shape, jnp.int32),
            pltpu.VMEM((16, 8, 128), f32),
            pltpu.VMEM((ROWS + 8, 128), f32),
            pltpu.SemaphoreType.DMA((8,)),
        ],
        compiler_params=params(61.75),
        cost_estimate=cost(2**17, 2**18),
    )(jnp.swapaxes(upper_inverse, 1, 2), row_samples.reshape(ROWS, 128), col_samples, pivot_rows, rank_blocks)
    rows = lax.all_gather(sent, "col", axis=0)
    packed = lax.all_to_all(packed.reshape(32, 4, 128), CHIPS + ("c",), 0, 0).reshape(128, 128)
    packed = jnp.concatenate([packed[8:], packed[0:2], packed[4:8]], axis=0)
    packed = lax.all_gather(packed, "col", axis=0)
    right = pl.pallas_call(
        right_kernel,
        in_specs=[vmem, vmem],
        out_specs=vmem,
        out_shape=jax.ShapeDtypeStruct((16, PAIRS, 4, 8, 128), f32),
        compiler_params=params(),
        cost_estimate=cost(2 * 3 * 128 * 2048 * 256, 5 * 2**20),
    )(packed, upanel_left[0])
    own = lax.all_to_all(right, CHIPS, 0, 0)
    other = lax.ppermute(own, "c", [(0, 1), (1, 0)])
    start, left, factor = first_call(rows, own)
    return second_call(factor, start, left, other)


def solution(mesh):
    chips = mesh.devices.reshape(4, 4, 2, 16)
    fine = Mesh(chips, ("y", "x", "c", "col"))
    row = ("y", "x", "c")
    in_specs = (
        P(row, None, "col", None),
        P(row, None, None, "col"),
        P(row, None),
        P(row),
        P(None, "col", row),
        P("col", None, None, None),
    )
    out_specs = (P(row, None, None, "col"), P(row, "col", None, None, None))
    return jax.shard_map(
        on_device, mesh=fine, in_specs=in_specs, out_specs=out_specs, check_vma=False
    )
```

```python
import functools

import jax
import jax.numpy as jnp
from jax import lax
from jax.experimental import pallas as pl
from jax.experimental.pallas import tpu as pltpu
from jax.sharding import Mesh
from jax.sharding import PartitionSpec as P

RANK_STEP = 16
CHIPS = ("y", "x")
DOWN_INVERSE, UP_INVERSE = 2.0 ** -16, 2.0 ** 16
DOWN_PRODUCT, UP_PRODUCT = 2.0 ** -24, 2.0 ** 24
PAIRS = 8
DEPTH = 2
ROWS = 512
BASE = 2 * PAIRS, 0


def params(mebibytes=24):
    return pltpu.CompilerParams(vmem_limit_bytes=int(mebibytes * 2**20))


def cost(flops, moved):
    return pl.CostEstimate(flops=flops, bytes_accessed=moved, transcendentals=0)


def split(x):
    high = x.astype(jnp.bfloat16)
    low = (x - high.astype(jnp.float32)).astype(jnp.bfloat16)
    return high, low


def dot(a, b):
    return jnp.dot(a, b, preferred_element_type=jnp.float32)


def sublanes(shape):
    return lax.broadcasted_iota(jnp.int32, shape, len(shape) - 2)


def interleave(even, odd):
    row = sublanes(even.shape)

    def turn(x, n):
        return jnp.roll(x, n, axis=x.ndim - 2)

    even2, odd2, even4, odd4, even6, odd6 = (turn(x, n) for n in (2, 4, 6) for x in (even, odd))
    low = jnp.where(row < 2, even, jnp.where(row < 4, odd2, jnp.where(row < 6, even2, odd4)))
    high = jnp.where(row < 2, even4, jnp.where(row < 4, odd6, jnp.where(row < 6, even6, odd)))
    return low, high


def start_kernel(
    block_hbm, rows_hbm, cols_hbm, pivots_hbm, ranks_hbm, out_hbm, sent_hbm, block_ref, cols_ref, pivots_ref, ranks_ref, out_ref, sent_ref, sems
):
    pairs = (
        (block_hbm, block_ref),
        (cols_hbm, cols_ref),
        (pivots_hbm, pivots_ref),
        (ranks_hbm, ranks_ref),
        (rows_hbm, sent_ref.at[0:ROWS]),
    )
    copies = [pltpu.make_async_copy(a, b, sems.at[n]) for n, (a, b) in enumerate(pairs)]
    for copy in copies:
        copy.start()
    copies[0].wait()
    rows = jnp.concatenate([block_ref[0].T, block_ref[1].T], axis=1).reshape(16, 8, 128)
    low, high = interleave(rows[:8], rows[8:])
    out_ref[0:8] = low
    out_ref[8:16] = high
    results = [
        pltpu.make_async_copy(out_ref, out_hbm, sems.at[5]),
        pltpu.make_async_copy(sent_ref.at[0:ROWS], sent_hbm.at[0:ROWS], sems.at[6]),
        pltpu.make_async_copy(sent_ref.at[ROWS : ROWS + 8], sent_hbm.at[ROWS : ROWS + 8], sems.at[7]),
    ]
    results[0].start()
    copies[4].wait()
    results[1].start()
    for copy in copies[1:4]:
        copy.wait()
    width = cols_ref.shape[2]
    levels = lax.broadcasted_iota(jnp.int32, (1, cols_ref.shape[3]), 1)
    rows = lax.broadcasted_iota(jnp.int32, cols_ref.shape[2:], 0) + lax.axis_index("col") * width
    for i in range(2):
        hit = jnp.logical_and(pivots_ref[i : i + 1, :] == rows, levels < RANK_STEP * ranks_ref[i])
        for p in range(2):
            at = ROWS + 2 * i + p
            sent_ref[at : at + 1, :] = jnp.sum(jnp.where(hit, cols_ref[i, p], 0.0), axis=0, keepdims=True)
    sent_ref[ROWS + 4 : ROWS + 8, :] = jnp.zeros((4, 128), jnp.float32)
    results[2].start()
    for result in results:
        result.wait()


def straight(x):
    lane = lax.broadcasted_iota(jnp.int32, x.shape, x.ndim - 1)
    same = (sublanes(x.shape) < 4) == (lane < 64)
    return jnp.where(same, x, jnp.roll(jnp.roll(x, 4, axis=x.ndim - 2), 64, axis=x.ndim - 1))


def right_kernel(rows_ref, left_ref, out_ref):
    place = lax.axis_index("col")
    last = rows_ref[0, 120:126, :]
    corner = straight(jnp.concatenate([last[0:2], jnp.zeros((2, 128), jnp.float32), last[2:6]], axis=0))
    total = None
    for q in range(16):
        if q == 0:
            x = jnp.concatenate([corner, jnp.zeros((120, 128), jnp.float32)], axis=0)
        else:
            x = straight(rows_ref[:, 8 * q - 8 : 8 * q, :]).reshape(128, 128)
        y = jnp.concatenate(
            [left_ref[0, 128 * q : 128 * q + 128, :], left_ref[1, 128 * q : 128 * q + 128, :]], axis=1
        )
        xh, xl = split(x)
        yh, yl = split(y * DOWN_PRODUCT)
        term = dot(xh, yh) + (dot(xh, yl) + dot(xl, yh))
        total = term if total is None else total + term
    by_real = total[:, :128].reshape(16, 8, 128)
    by_imag = jnp.roll(total[:, 128:].reshape(16, 8, 128), 4, axis=1)
    product = by_real + jnp.where(sublanes((16, 8, 128)) < 4, -by_imag, by_imag)
    start = pl.multiple_of(jnp.maximum(place - 1, 0) * 8, 8)
    block = straight(rows_ref[:, pl.ds(start, 8), :])
    which = lax.broadcasted_iota(jnp.int32, (16, 8, 128), 0)
    block = jnp.where(place == 0, jnp.where(which == 0, corner[None], 0.0), block)
    for n, x in enumerate((block * DOWN_INVERSE, product)):
        x = x.reshape(PAIRS, 2, 8, 128)
        real, imag = interleave(x[:, 0], x[:, 1])
        pair = jnp.stack([real, imag], axis=1).reshape(2 * PAIRS, 8, 128)
        for d in range(16):
            out_ref[d, BASE[n] : BASE[n] + 2 * PAIRS] = pair


def tiles(block):
    first = sublanes((8, 8, 128)) < 4
    low, high = block[0:8], block[8:16]
    pair = (jnp.where(first, low, jnp.roll(high, 4, axis=1)), jnp.where(first, jnp.roll(low, 4, axis=1), high))
    return jnp.concatenate(pair, axis=0).reshape(128, 128)


def dot3(left, right):
    return dot(left[0], right[0]) + (dot(left[0], right[1]) + dot(left[1], right[0]))


def first_kernel(rows_ref, right_ref, out_ref, later_ref, factor_ref, held_ref, high_ref, low_ref, sems):
    copies = [pltpu.make_async_copy(rows_ref.at[z], held_ref.at[z], sems.at[z]) for z in range(16)]
    for copy in copies:
        copy.start()
    core = lax.axis_index("c")
    shift = jnp.where(core == 0, 2, 126)
    keep = ((lax.broadcasted_iota(jnp.int32, (128, 128), 1) & 3) < 2) == (core == 0)
    for n in range(PAIRS):
        right = jnp.concatenate([tiles(right_ref[:, BASE[m // 2] + 2 * n + m % 2]) for m in range(4)], axis=1)
        high_ref[128 * n : 128 * n + 128, :], low_ref[128 * n : 128 * n + 128, :] = split(right)
    total = None
    for step in range(PAIRS // DEPTH):
        lefts = []
        for n in range(step * DEPTH, step * DEPTH + DEPTH):
            copies[2 * n].wait()
            copies[2 * n + 1].wait()
            blocks = []
            for p in range(2):
                for i in range(2):
                    at = slice(256 * i + 128 * p, 256 * i + 128 * p + 128)
                    near, far = held_ref[2 * n + core, at], held_ref[2 * n + 1 - core, at]
                    blocks.append(jnp.where(keep, near, pltpu.roll(far, shift, 1)))
                    high, low = split(jnp.where(keep, pltpu.roll(near, 128 - shift, 1), far))
                    span = slice(256 * p + 128 * i, 256 * p + 128 * i + 128)
                    later_ref[0, span, 128 * n : 128 * n + 128] = high
                    later_ref[1, span, 128 * n : 128 * n + 128] = low
            lefts.append(jnp.concatenate(blocks, axis=0))
        at = slice(128 * DEPTH * step, 128 * DEPTH * step + 128 * DEPTH)
        term = dot3(split(jnp.concatenate(lefts, axis=1)), (high_ref[at, :], low_ref[at, :]))
        total = term if total is None else total + term
    out_ref[...] = total
    entries = jnp.sum(held_ref[:, ROWS : ROWS + 8], axis=0)
    for i in range(2):
        real, imag = entries[2 * i : 2 * i + 1], entries[2 * i + 1 : 2 * i + 2]
        magnitude = jnp.maximum(real * real + imag * imag, 1.0)
        factor_ref[2 * i : 2 * i + 1, :] = real / magnitude
        factor_ref[2 * i + 1 : 2 * i + 2, :] = -imag / magnitude
    factor_ref[4:8, :] = jnp.zeros((4, 128), jnp.float32)


def second_kernel(
    factor_ref,
    start_ref,
    left_ref,
    right_ref,
    panel_ref,
    cores_ref,
    near_ref,
    high_ref,
    low_ref,
    panel_vmem,
    cores_vmem,
    sems,
    out_sems,
):
    copies = [
        [
            pltpu.make_async_copy(
                right_ref.at[:, BASE[n] + 2 * z : BASE[n] + 2 * z + 2], near_ref.at[n, z], sems.at[n, z]
            )
            for z in range(PAIRS)
        ]
        for n in range(2)
    ]
    for copy in copies[0] + copies[1]:
        copy.start()
    columns = factor_ref[...].T
    results = (
        (pltpu.make_async_copy(panel_vmem, panel_ref, out_sems.at[0]), panel_vmem, UP_INVERSE),
        (pltpu.make_async_copy(cores_vmem, cores_ref, out_sems.at[1]), cores_vmem, UP_PRODUCT),
    )
    def ready(n):
        for z in range(PAIRS):
            copies[n][z].wait()
            right = jnp.concatenate([tiles(near_ref[n, z, :, p]) for p in range(2)], axis=1)
            high_ref[n, 128 * z : 128 * z + 128, :], low_ref[n, 128 * z : 128 * z + 128, :] = split(right)

    ready(0)
    ready(1)
    for n, (result, out, up) in enumerate(results):
        total = start_ref[:, 256 * n : 256 * n + 256] + dot3(left_ref, (high_ref[n], low_ref[n]))
        for i in range(2):
            fr, fi = columns[:, 2 * i : 2 * i + 1], columns[:, 2 * i + 1 : 2 * i + 2]
            by_real, by_imag = total[128 * i : 128 * i + 128], total[256 + 128 * i : 384 + 128 * i]
            real = by_real[:, :128] - by_imag[:, 128:]
            imag = by_real[:, 128:] + by_imag[:, :128]
            where = (i,) if n == 0 else (i, 0)
            out[where + (0,)] = (fr * real - fi * imag) * up
            out[where + (1,)] = (fr * imag + fi * real) * up
        result.start()
    for result, _, _ in results:
        result.wait()


def first_call(rows, right):
    vmem = pl.BlockSpec(memory_space=pltpu.VMEM)
    return pl.pallas_call(
        first_kernel,
        in_specs=[pl.BlockSpec(memory_space=pltpu.HBM), vmem],
        out_specs=(vmem, vmem, vmem),
        out_shape=(
            jax.ShapeDtypeStruct((512, 512), jnp.float32),
            jax.ShapeDtypeStruct((2, 512, 1024), jnp.bfloat16),
            jax.ShapeDtypeStruct((8, 128), jnp.float32),
        ),
        scratch_shapes=[
            pltpu.VMEM((16, ROWS + 8, 128), jnp.float32),
            pltpu.VMEM((1024, 512), jnp.bfloat16),
            pltpu.VMEM((1024, 512), jnp.bfloat16),
            pltpu.SemaphoreType.DMA((16,)),
        ],
        compiler_params=params(48),
        cost_estimate=cost(2 * 3 * 512 * 1024 * 512, 7 * 2**20),
    )(rows, right)


def second_call(factor, start, left, right):
    vmem = pl.BlockSpec(memory_space=pltpu.VMEM)
    hbm = pl.BlockSpec(memory_space=pltpu.HBM)
    shapes = (2, 2, 128, 128), (2, 1, 2, 128, 128)
    return pl.pallas_call(
        second_kernel,
        in_specs=[vmem, vmem, vmem, hbm],
        out_specs=(hbm, hbm),
        out_shape=tuple(jax.ShapeDtypeStruct(shape, jnp.float32) for shape in shapes),
        scratch_shapes=[
            pltpu.VMEM((2, PAIRS, 16, 2, 8, 128), jnp.float32),
            pltpu.VMEM((2, 1024, 256), jnp.bfloat16),
            pltpu.VMEM((2, 1024, 256), jnp.bfloat16),
            pltpu.VMEM(shapes[0], jnp.float32),
            pltpu.VMEM(shapes[1], jnp.float32),
            pltpu.SemaphoreType.DMA((2, PAIRS)),
            pltpu.SemaphoreType.DMA((2,)),
        ],
        compiler_params=params(48),
        cost_estimate=cost(2 * 3 * 512 * 1024 * 512, 8 * 2**20),
    )(factor, start, left, right)


def spread(pairs, right):
    count = 2 * PAIRS + 2 * pairs
    got = lax.all_to_all(right[:, :count], CHIPS, 0, 0)
    return jnp.pad(got, ((0, 0), (0, right.shape[1] - count), (0, 0), (0, 0)))


def on_device(col_samples, row_samples, pivot_rows, rank_blocks, upper_inverse, upanel_left):
    f32 = jnp.float32
    vmem = pl.BlockSpec(memory_space=pltpu.VMEM)
    hbm = pl.BlockSpec(memory_space=pltpu.HBM)
    packed, sent = pl.pallas_call(
        start_kernel,
        in_specs=[hbm] * 5,
        out_specs=(hbm, hbm),
        out_shape=(jax.ShapeDtypeStruct((16, 8, 128), f32), jax.ShapeDtypeStruct((ROWS + 8, 128), f32)),
        scratch_shapes=[
            pltpu.VMEM((2, 64, 128), f32),
            pltpu.VMEM(col_samples.shape, f32),
            pltpu.VMEM(pivot_rows.shape, jnp.int32),
            pltpu.SMEM(rank_blocks.shape, jnp.int32),
            pltpu.VMEM((16, 8, 128), f32),
            pltpu.VMEM((ROWS + 8, 128), f32),
            pltpu.SemaphoreType.DMA((8,)),
        ],
        compiler_params=params(61.75),
        cost_estimate=cost(2**17, 2**18),
    )(jnp.swapaxes(upper_inverse, 1, 2), row_samples.reshape(ROWS, 128), col_samples, pivot_rows, rank_blocks)
    rows = lax.all_gather(sent, "col", axis=0)
    packed = lax.all_to_all(packed.reshape(32, 4, 128), CHIPS + ("c",), 0, 0).reshape(128, 128)
    packed = jnp.concatenate([packed[8:], packed[0:2], packed[4:8]], axis=0)
    packed = lax.all_gather(packed, "col", axis=0)
    right = pl.pallas_call(
        right_kernel,
        in_specs=[vmem, vmem],
        out_specs=vmem,
        out_shape=jax.ShapeDtypeStruct((16, 4 * PAIRS, 8, 128), f32),
        compiler_params=params(),
        cost_estimate=cost(2 * 3 * 128 * 2048 * 256, 5 * 2**20),
    )(packed, upanel_left[0])
    place = lax.axis_index("col")
    kind = (place >= 4).astype(jnp.int32) + (place >= 8).astype(jnp.int32)
    own = lax.switch(kind, [functools.partial(spread, pairs) for pairs in (2, 4, 8)], right)
    other = lax.ppermute(own, "c", [(0, 1), (1, 0)])
    start, left, factor = first_call(rows, own)
    return second_call(factor, start, left, other)


def solution(mesh):
    chips = mesh.devices.reshape(4, 4, 2, 16)
    fine = Mesh(chips, ("y", "x", "c", "col"))
    row = ("y", "x", "c")
    in_specs = (
        P(row, None, "col", None),
        P(row, None, None, "col"),
        P(row, None),
        P(row),
        P(None, "col", row),
        P("col", None, None, None),
    )
    out_specs = (P(row, None, None, "col"), P(row, "col", None, None, None))
    return jax.shard_map(
        on_device, mesh=fine, in_specs=in_specs, out_specs=out_specs, check_vma=False
    )
```

```python
import functools

import jax
import jax.numpy as jnp
from jax import lax
from jax.experimental import pallas as pl
from jax.experimental.pallas import tpu as pltpu
from jax.sharding import Mesh
from jax.sharding import PartitionSpec as P

RANK_STEP = 16
CHIPS = ("y", "x")
DOWN_INVERSE, UP_INVERSE = 2.0 ** -16, 2.0 ** 16
DOWN_PRODUCT, UP_PRODUCT = 2.0 ** -24, 2.0 ** 24
PAIRS = 8
DEPTH = 2
ROWS = 512
BASE = 2 * PAIRS, 0


def params(mebibytes=24):
    return pltpu.CompilerParams(vmem_limit_bytes=int(mebibytes * 2**20))


def cost(flops, moved):
    return pl.CostEstimate(flops=flops, bytes_accessed=moved, transcendentals=0)


def split(x):
    high = x.astype(jnp.bfloat16)
    low = (x - high.astype(jnp.float32)).astype(jnp.bfloat16)
    return high, low


def dot(a, b):
    return jnp.dot(a, b, preferred_element_type=jnp.float32)


def sublanes(shape):
    return lax.broadcasted_iota(jnp.int32, shape, len(shape) - 2)


def interleave(even, odd):
    row = sublanes(even.shape)

    def turn(x, n):
        return jnp.roll(x, n, axis=x.ndim - 2)

    even2, odd2, even4, odd4, even6, odd6 = (turn(x, n) for n in (2, 4, 6) for x in (even, odd))
    low = jnp.where(row < 2, even, jnp.where(row < 4, odd2, jnp.where(row < 6, even2, odd4)))
    high = jnp.where(row < 2, even4, jnp.where(row < 4, odd6, jnp.where(row < 6, even6, odd)))
    return low, high


def start_kernel(
    block_hbm, rows_hbm, cols_hbm, pivots_hbm, ranks_hbm, out_hbm, sent_hbm, block_ref, cols_ref, pivots_ref, ranks_ref, out_ref, sent_ref, sems
):
    pairs = (
        (block_hbm, block_ref),
        (cols_hbm, cols_ref),
        (pivots_hbm, pivots_ref),
        (ranks_hbm, ranks_ref),
        (rows_hbm, sent_ref.at[0:ROWS]),
    )
    copies = [pltpu.make_async_copy(a, b, sems.at[n]) for n, (a, b) in enumerate(pairs)]
    for copy in copies:
        copy.start()
    copies[0].wait()
    rows = jnp.concatenate([block_ref[0].T, block_ref[1].T], axis=1).reshape(16, 8, 128)
    low, high = interleave(rows[:8], rows[8:])
    out_ref[0:8] = low
    out_ref[8:16] = high
    results = [
        pltpu.make_async_copy(out_ref, out_hbm, sems.at[5]),
        pltpu.make_async_copy(sent_ref.at[0:ROWS], sent_hbm.at[0:ROWS], sems.at[6]),
        pltpu.make_async_copy(sent_ref.at[ROWS : ROWS + 8], sent_hbm.at[ROWS : ROWS + 8], sems.at[7]),
    ]
    results[0].start()
    copies[4].wait()
    results[1].start()
    for copy in copies[1:4]:
        copy.wait()
    width = cols_ref.shape[2]
    levels = lax.broadcasted_iota(jnp.int32, (1, cols_ref.shape[3]), 1)
    rows = lax.broadcasted_iota(jnp.int32, cols_ref.shape[2:], 0) + lax.axis_index("col") * width
    for i in range(2):
        hit = jnp.logical_and(pivots_ref[i : i + 1, :] == rows, levels < RANK_STEP * ranks_ref[i])
        for p in range(2):
            at = ROWS + 2 * i + p
            sent_ref[at : at + 1, :] = jnp.sum(jnp.where(hit, cols_ref[i, p], 0.0), axis=0, keepdims=True)
    sent_ref[ROWS + 4 : ROWS + 8, :] = jnp.zeros((4, 128), jnp.float32)
    results[2].start()
    for result in results:
        result.wait()


def straight(x):
    lane = lax.broadcasted_iota(jnp.int32, x.shape, x.ndim - 1)
    same = (sublanes(x.shape) < 4) == (lane < 64)
    return jnp.where(same, x, jnp.roll(jnp.roll(x, 4, axis=x.ndim - 2), 64, axis=x.ndim - 1))


def right_kernel(rows_ref, left_ref, out_ref):
    place = lax.axis_index("col")
    last = rows_ref[0, 120:126, :]
    corner = straight(jnp.concatenate([last[0:2], jnp.zeros((2, 128), jnp.float32), last[2:6]], axis=0))
    total = None
    for q in range(16):
        if q == 0:
            x = jnp.concatenate([corner, jnp.zeros((120, 128), jnp.float32)], axis=0)
        else:
            x = straight(rows_ref[:, 8 * q - 8 : 8 * q, :]).reshape(128, 128)
        y = jnp.concatenate(
            [left_ref[0, 128 * q : 128 * q + 128, :], left_ref[1, 128 * q : 128 * q + 128, :]], axis=1
        )
        xh, xl = split(x)
        yh, yl = split(y * DOWN_PRODUCT)
        term = dot(xh, yh) + (dot(xh, yl) + dot(xl, yh))
        total = term if total is None else total + term
    by_real = total[:, :128].reshape(16, 8, 128)
    by_imag = jnp.roll(total[:, 128:].reshape(16, 8, 128), 4, axis=1)
    product = by_real + jnp.where(sublanes((16, 8, 128)) < 4, -by_imag, by_imag)
    start = pl.multiple_of(jnp.maximum(place - 1, 0) * 8, 8)
    block = straight(rows_ref[:, pl.ds(start, 8), :])
    which = lax.broadcasted_iota(jnp.int32, (16, 8, 128), 0)
    block = jnp.where(place == 0, jnp.where(which == 0, corner[None], 0.0), block)
    for n, x in enumerate((block * DOWN_INVERSE, product)):
        x = x.reshape(PAIRS, 2, 8, 128)
        real, imag = interleave(x[:, 0], x[:, 1])
        pair = jnp.stack([real, imag], axis=1).reshape(2 * PAIRS, 8, 128)
        for d in range(16):
            out_ref[d, BASE[n] : BASE[n] + 2 * PAIRS] = pair


def tiles(block):
    first = sublanes((8, 8, 128)) < 4
    low, high = block[0:8], block[8:16]
    pair = (jnp.where(first, low, jnp.roll(high, 4, axis=1)), jnp.where(first, jnp.roll(low, 4, axis=1), high))
    return jnp.concatenate(pair, axis=0).reshape(128, 128)


def dot3(left, right):
    return dot(left[0], right[0]) + (dot(left[0], right[1]) + dot(left[1], right[0]))


def first_kernel(rows_ref, right_ref, out_ref, later_ref, factor_ref, held_ref, near_ref, high_ref, low_ref, sems, near_sems):
    nears = [
        [
            pltpu.make_async_copy(
                right_ref.at[:, BASE[m] + 2 * n : BASE[m] + 2 * n + 2], near_ref.at[m, n], near_sems.at[m, n]
            )
            for m in range(2)
        ]
        for n in range(PAIRS)
    ]
    for pair in nears:
        for copy in pair:
            copy.start()
    copies = [pltpu.make_async_copy(rows_ref.at[z], held_ref.at[z], sems.at[z]) for z in range(16)]
    for copy in copies:
        copy.start()
    core = lax.axis_index("c")
    shift = jnp.where(core == 0, 2, 126)
    keep = ((lax.broadcasted_iota(jnp.int32, (128, 128), 1) & 3) < 2) == (core == 0)
    for n in range(PAIRS):
        for copy in nears[n]:
            copy.wait()
        right = jnp.concatenate([tiles(near_ref[m // 2, n, :, m % 2]) for m in range(4)], axis=1)
        high_ref[128 * n : 128 * n + 128, :], low_ref[128 * n : 128 * n + 128, :] = split(right)
    total = None
    for step in range(PAIRS // DEPTH):
        lefts = []
        for n in range(step * DEPTH, step * DEPTH + DEPTH):
            copies[2 * n].wait()
            copies[2 * n + 1].wait()
            blocks = []
            for p in range(2):
                for i in range(2):
                    at = slice(256 * i + 128 * p, 256 * i + 128 * p + 128)
                    near, far = held_ref[2 * n + core, at], held_ref[2 * n + 1 - core, at]
                    blocks.append(jnp.where(keep, near, pltpu.roll(far, shift, 1)))
                    high, low = split(jnp.where(keep, pltpu.roll(near, 128 - shift, 1), far))
                    span = slice(256 * p + 128 * i, 256 * p + 128 * i + 128)
                    later_ref[0, span, 128 * n : 128 * n + 128] = high
                    later_ref[1, span, 128 * n : 128 * n + 128] = low
            lefts.append(jnp.concatenate(blocks, axis=0))
        at = slice(128 * DEPTH * step, 128 * DEPTH * step + 128 * DEPTH)
        term = dot3(split(jnp.concatenate(lefts, axis=1)), (high_ref[at, :], low_ref[at, :]))
        total = term if total is None else total + term
    out_ref[...] = total
    entries = jnp.sum(held_ref[:, ROWS : ROWS + 8], axis=0)
    for i in range(2):
        real, imag = entries[2 * i : 2 * i + 1], entries[2 * i + 1 : 2 * i + 2]
        magnitude = jnp.maximum(real * real + imag * imag, 1.0)
        factor_ref[2 * i : 2 * i + 1, :] = real / magnitude
        factor_ref[2 * i + 1 : 2 * i + 2, :] = -imag / magnitude
    factor_ref[4:8, :] = jnp.zeros((4, 128), jnp.float32)


def second_kernel(
    factor_ref,
    start_ref,
    left_ref,
    right_ref,
    panel_ref,
    cores_ref,
    near_ref,
    high_ref,
    low_ref,
    panel_vmem,
    cores_vmem,
    sems,
    out_sems,
):
    copies = [
        [
            pltpu.make_async_copy(
                right_ref.at[:, BASE[n] + 2 * z : BASE[n] + 2 * z + 2], near_ref.at[n, z], sems.at[n, z]
            )
            for z in range(PAIRS)
        ]
        for n in range(2)
    ]
    for copy in copies[0] + copies[1]:
        copy.start()
    columns = factor_ref[...].T
    results = (
        (pltpu.make_async_copy(panel_vmem, panel_ref, out_sems.at[0]), panel_vmem, UP_INVERSE),
        (pltpu.make_async_copy(cores_vmem, cores_ref, out_sems.at[1]), cores_vmem, UP_PRODUCT),
    )
    def ready(n):
        for z in range(PAIRS):
            copies[n][z].wait()
            right = jnp.concatenate([tiles(near_ref[n, z, :, p]) for p in range(2)], axis=1)
            high_ref[n, 128 * z : 128 * z + 128, :], low_ref[n, 128 * z : 128 * z + 128, :] = split(right)

    ready(0)
    ready(1)
    for n, (result, out, up) in enumerate(results):
        total = start_ref[:, 256 * n : 256 * n + 256] + dot3(left_ref, (high_ref[n], low_ref[n]))
        for i in range(2):
            fr, fi = columns[:, 2 * i : 2 * i + 1], columns[:, 2 * i + 1 : 2 * i + 2]
            by_real, by_imag = total[128 * i : 128 * i + 128], total[256 + 128 * i : 384 + 128 * i]
            real = by_real[:, :128] - by_imag[:, 128:]
            imag = by_real[:, 128:] + by_imag[:, :128]
            where = (i,) if n == 0 else (i, 0)
            out[where + (0,)] = (fr * real - fi * imag) * up
            out[where + (1,)] = (fr * imag + fi * real) * up
        result.start()
    for result, _, _ in results:
        result.wait()


def first_call(rows, right):
    vmem = pl.BlockSpec(memory_space=pltpu.VMEM)
    return pl.pallas_call(
        first_kernel,
        in_specs=[pl.BlockSpec(memory_space=pltpu.HBM)] * 2,
        out_specs=(vmem, vmem, vmem),
        out_shape=(
            jax.ShapeDtypeStruct((512, 512), jnp.float32),
            jax.ShapeDtypeStruct((2, 512, 1024), jnp.bfloat16),
            jax.ShapeDtypeStruct((8, 128), jnp.float32),
        ),
        scratch_shapes=[
            pltpu.VMEM((16, ROWS + 8, 128), jnp.float32),
            pltpu.VMEM((2, PAIRS, 16, 2, 8, 128), jnp.float32),
            pltpu.VMEM((1024, 512), jnp.bfloat16),
            pltpu.VMEM((1024, 512), jnp.bfloat16),
            pltpu.SemaphoreType.DMA((16,)),
            pltpu.SemaphoreType.DMA((2, PAIRS)),
        ],
        compiler_params=params(48),
        cost_estimate=cost(2 * 3 * 512 * 1024 * 512, 7 * 2**20),
    )(rows, right)


def second_call(factor, start, left, right):
    vmem = pl.BlockSpec(memory_space=pltpu.VMEM)
    hbm = pl.BlockSpec(memory_space=pltpu.HBM)
    shapes = (2, 2, 128, 128), (2, 1, 2, 128, 128)
    return pl.pallas_call(
        second_kernel,
        in_specs=[vmem, vmem, vmem, hbm],
        out_specs=(hbm, hbm),
        out_shape=tuple(jax.ShapeDtypeStruct(shape, jnp.float32) for shape in shapes),
        scratch_shapes=[
            pltpu.VMEM((2, PAIRS, 16, 2, 8, 128), jnp.float32),
            pltpu.VMEM((2, 1024, 256), jnp.bfloat16),
            pltpu.VMEM((2, 1024, 256), jnp.bfloat16),
            pltpu.VMEM(shapes[0], jnp.float32),
            pltpu.VMEM(shapes[1], jnp.float32),
            pltpu.SemaphoreType.DMA((2, PAIRS)),
            pltpu.SemaphoreType.DMA((2,)),
        ],
        compiler_params=params(48),
        cost_estimate=cost(2 * 3 * 512 * 1024 * 512, 8 * 2**20),
    )(factor, start, left, right)


def spread(pairs, right):
    count = 2 * PAIRS + 2 * pairs
    got = lax.all_to_all(right[:, :count], CHIPS, 0, 0)
    return jnp.pad(got, ((0, 0), (0, right.shape[1] - count), (0, 0), (0, 0)))


def on_device(col_samples, row_samples, pivot_rows, rank_blocks, upper_inverse, upanel_left):
    f32 = jnp.float32
    vmem = pl.BlockSpec(memory_space=pltpu.VMEM)
    hbm = pl.BlockSpec(memory_space=pltpu.HBM)
    packed, sent = pl.pallas_call(
        start_kernel,
        in_specs=[hbm] * 5,
        out_specs=(hbm, hbm),
        out_shape=(jax.ShapeDtypeStruct((16, 8, 128), f32), jax.ShapeDtypeStruct((ROWS + 8, 128), f32)),
        scratch_shapes=[
            pltpu.VMEM((2, 64, 128), f32),
            pltpu.VMEM(col_samples.shape, f32),
            pltpu.VMEM(pivot_rows.shape, jnp.int32),
            pltpu.SMEM(rank_blocks.shape, jnp.int32),
            pltpu.VMEM((16, 8, 128), f32),
            pltpu.VMEM((ROWS + 8, 128), f32),
            pltpu.SemaphoreType.DMA((8,)),
        ],
        compiler_params=params(61.75),
        cost_estimate=cost(2**17, 2**18),
    )(jnp.swapaxes(upper_inverse, 1, 2), row_samples.reshape(ROWS, 128), col_samples, pivot_rows, rank_blocks)
    rows = lax.all_gather(sent, "col", axis=0)
    packed = lax.all_to_all(packed.reshape(32, 4, 128), CHIPS + ("c",), 0, 0).reshape(128, 128)
    packed = jnp.concatenate([packed[8:], packed[0:2], packed[4:8]], axis=0)
    packed = lax.all_gather(packed, "col", axis=0)
    right = pl.pallas_call(
        right_kernel,
        in_specs=[vmem, vmem],
        out_specs=vmem,
        out_shape=jax.ShapeDtypeStruct((16, 4 * PAIRS, 8, 128), f32),
        compiler_params=params(),
        cost_estimate=cost(2 * 3 * 128 * 2048 * 256, 5 * 2**20),
    )(packed, upanel_left[0])
    place = lax.axis_index("col")
    sizes = 1, 2, 4, 6, PAIRS
    kind = sum((place >= 2 * pairs).astype(jnp.int32) for pairs in sizes[:-1])
    own = lax.switch(kind, [functools.partial(spread, pairs) for pairs in sizes], right)
    other = lax.ppermute(own, "c", [(0, 1), (1, 0)])
    start, left, factor = first_call(rows, own)
    return second_call(factor, start, left, other)


def solution(mesh):
    chips = mesh.devices.reshape(4, 4, 2, 16)
    fine = Mesh(chips, ("y", "x", "c", "col"))
    row = ("y", "x", "c")
    in_specs = (
        P(row, None, "col", None),
        P(row, None, None, "col"),
        P(row, None),
        P(row),
        P(None, "col", row),
        P("col", None, None, None),
    )
    out_specs = (P(row, None, None, "col"), P(row, "col", None, None, None))
    return jax.shard_map(
        on_device, mesh=fine, in_specs=in_specs, out_specs=out_specs, check_vma=False
    )
```

```python
import functools

import jax
import jax.numpy as jnp
from jax import lax
from jax.experimental import pallas as pl
from jax.experimental.pallas import tpu as pltpu
from jax.sharding import Mesh
from jax.sharding import PartitionSpec as P

RANK_STEP = 16
CHIPS = ("y", "x")
DOWN_INVERSE, UP_INVERSE = 2.0 ** -16, 2.0 ** 16
DOWN_PRODUCT, UP_PRODUCT = 2.0 ** -24, 2.0 ** 24
PAIRS = 8
DEPTH = 2
ROWS = 512
BASE = 2 * PAIRS, 0


def params(mebibytes=24):
    return pltpu.CompilerParams(vmem_limit_bytes=int(mebibytes * 2**20))


def cost(flops, moved):
    return pl.CostEstimate(flops=flops, bytes_accessed=moved, transcendentals=0)


def split(x):
    high = x.astype(jnp.bfloat16)
    low = (x - high.astype(jnp.float32)).astype(jnp.bfloat16)
    return high, low


def dot(a, b):
    return jnp.dot(a, b, preferred_element_type=jnp.float32)


def sublanes(shape):
    return lax.broadcasted_iota(jnp.int32, shape, len(shape) - 2)


def interleave(even, odd):
    row = sublanes(even.shape)

    def turn(x, n):
        return jnp.roll(x, n, axis=x.ndim - 2)

    even2, odd2, even4, odd4, even6, odd6 = (turn(x, n) for n in (2, 4, 6) for x in (even, odd))
    low = jnp.where(row < 2, even, jnp.where(row < 4, odd2, jnp.where(row < 6, even2, odd4)))
    high = jnp.where(row < 2, even4, jnp.where(row < 4, odd6, jnp.where(row < 6, even6, odd)))
    return low, high


def start_kernel(
    block_hbm, rows_hbm, cols_hbm, pivots_hbm, ranks_hbm, out_hbm, sent_hbm, block_ref, cols_ref, pivots_ref, ranks_ref, out_ref, sent_ref, sems
):
    pairs = (
        (block_hbm, block_ref),
        (cols_hbm, cols_ref),
        (pivots_hbm, pivots_ref),
        (ranks_hbm, ranks_ref),
        (rows_hbm, sent_ref.at[0:ROWS]),
    )
    copies = [pltpu.make_async_copy(a, b, sems.at[n]) for n, (a, b) in enumerate(pairs)]
    for copy in copies:
        copy.start()
    copies[0].wait()
    rows = jnp.concatenate([block_ref[0].T, block_ref[1].T], axis=1).reshape(16, 8, 128)
    low, high = interleave(rows[:8], rows[8:])
    out_ref[0:8] = low
    out_ref[8:16] = high
    results = [
        pltpu.make_async_copy(out_ref, out_hbm, sems.at[5]),
        pltpu.make_async_copy(sent_ref.at[0:ROWS], sent_hbm.at[0:ROWS], sems.at[6]),
        pltpu.make_async_copy(sent_ref.at[ROWS : ROWS + 8], sent_hbm.at[ROWS : ROWS + 8], sems.at[7]),
    ]
    results[0].start()
    copies[4].wait()
    results[1].start()
    for copy in copies[1:4]:
        copy.wait()
    width = cols_ref.shape[2]
    levels = lax.broadcasted_iota(jnp.int32, (1, cols_ref.shape[3]), 1)
    rows = lax.broadcasted_iota(jnp.int32, cols_ref.shape[2:], 0) + lax.axis_index("col") * width
    for i in range(2):
        hit = jnp.logical_and(pivots_ref[i : i + 1, :] == rows, levels < RANK_STEP * ranks_ref[i])
        for p in range(2):
            at = ROWS + 2 * i + p
            sent_ref[at : at + 1, :] = jnp.sum(jnp.where(hit, cols_ref[i, p], 0.0), axis=0, keepdims=True)
    sent_ref[ROWS + 4 : ROWS + 8, :] = jnp.zeros((4, 128), jnp.float32)
    results[2].start()
    for result in results:
        result.wait()


def straight(x):
    lane = lax.broadcasted_iota(jnp.int32, x.shape, x.ndim - 1)
    same = (sublanes(x.shape) < 4) == (lane < 64)
    return jnp.where(same, x, jnp.roll(jnp.roll(x, 4, axis=x.ndim - 2), 64, axis=x.ndim - 1))


def right_kernel(rows_ref, left_ref, out_ref):
    place = lax.axis_index("col")
    last = rows_ref[0, 120:126, :]
    corner = straight(jnp.concatenate([last[0:2], jnp.zeros((2, 128), jnp.float32), last[2:6]], axis=0))
    total = None
    for q in range(16):
        if q == 0:
            x = jnp.concatenate([corner, jnp.zeros((120, 128), jnp.float32)], axis=0)
        else:
            x = straight(rows_ref[:, 8 * q - 8 : 8 * q, :]).reshape(128, 128)
        y = jnp.concatenate(
            [left_ref[0, 128 * q : 128 * q + 128, :], left_ref[1, 128 * q : 128 * q + 128, :]], axis=1
        )
        xh, xl = split(x)
        yh, yl = split(y * DOWN_PRODUCT)
        term = dot(xh, yh) + (dot(xh, yl) + dot(xl, yh))
        total = term if total is None else total + term
    by_real = total[:, :128].reshape(16, 8, 128)
    by_imag = jnp.roll(total[:, 128:].reshape(16, 8, 128), 4, axis=1)
    product = by_real + jnp.where(sublanes((16, 8, 128)) < 4, -by_imag, by_imag)
    start = pl.multiple_of(jnp.maximum(place - 1, 0) * 8, 8)
    block = straight(rows_ref[:, pl.ds(start, 8), :])
    which = lax.broadcasted_iota(jnp.int32, (16, 8, 128), 0)
    block = jnp.where(place == 0, jnp.where(which == 0, corner[None], 0.0), block)
    for n, x in enumerate((block * DOWN_INVERSE, product)):
        x = x.reshape(PAIRS, 2, 8, 128)
        real, imag = interleave(x[:, 0], x[:, 1])
        pair = jnp.stack([real, imag], axis=1).reshape(2 * PAIRS, 8, 128)
        for d in range(16):
            out_ref[d, BASE[n] : BASE[n] + 2 * PAIRS] = pair


def tiles(block):
    first = sublanes((8, 8, 128)) < 4
    low, high = block[0:8], block[8:16]
    pair = (jnp.where(first, low, jnp.roll(high, 4, axis=1)), jnp.where(first, jnp.roll(low, 4, axis=1), high))
    return jnp.concatenate(pair, axis=0).reshape(128, 128)


def dot3(left, right):
    return dot(left[0], right[0]) + (dot(left[0], right[1]) + dot(left[1], right[0]))


def first_kernel(rows_ref, right_ref, out_ref, later_ref, factor_ref, held_ref, high_ref, low_ref, sems):
    copies = [pltpu.make_async_copy(rows_ref.at[z], held_ref.at[z], sems.at[z]) for z in range(16)]
    for copy in copies:
        copy.start()
    core = lax.axis_index("c")
    shift = jnp.where(core == 0, 2, 126)
    keep = ((lax.broadcasted_iota(jnp.int32, (128, 128), 1) & 3) < 2) == (core == 0)
    for n in range(PAIRS):
        right = jnp.concatenate([tiles(right_ref[:, BASE[m // 2] + 2 * n + m % 2]) for m in range(4)], axis=1)
        high_ref[128 * n : 128 * n + 128, :], low_ref[128 * n : 128 * n + 128, :] = split(right)
    total = None
    for step in range(PAIRS // DEPTH):
        lefts = []
        for n in range(step * DEPTH, step * DEPTH + DEPTH):
            copies[2 * n].wait()
            copies[2 * n + 1].wait()
            blocks = []
            for p in range(2):
                for i in range(2):
                    at = slice(256 * i + 128 * p, 256 * i + 128 * p + 128)
                    near, far = held_ref[2 * n + core, at], held_ref[2 * n + 1 - core, at]
                    blocks.append(jnp.where(keep, near, pltpu.roll(far, shift, 1)))
                    high, low = split(jnp.where(keep, pltpu.roll(near, 128 - shift, 1), far))
                    span = slice(256 * p + 128 * i, 256 * p + 128 * i + 128)
                    later_ref[0, span, 128 * n : 128 * n + 128] = high
                    later_ref[1, span, 128 * n : 128 * n + 128] = low
            lefts.append(jnp.concatenate(blocks, axis=0))
        at = slice(128 * DEPTH * step, 128 * DEPTH * step + 128 * DEPTH)
        term = dot3(split(jnp.concatenate(lefts, axis=1)), (high_ref[at, :], low_ref[at, :]))
        total = term if total is None else total + term
    out_ref[...] = total
    entries = jnp.sum(held_ref[:, ROWS : ROWS + 8], axis=0)
    for i in range(2):
        real, imag = entries[2 * i : 2 * i + 1], entries[2 * i + 1 : 2 * i + 2]
        magnitude = jnp.maximum(real * real + imag * imag, 1.0)
        factor_ref[2 * i : 2 * i + 1, :] = real / magnitude
        factor_ref[2 * i + 1 : 2 * i + 2, :] = -imag / magnitude
    factor_ref[4:8, :] = jnp.zeros((4, 128), jnp.float32)


def second_kernel(
    factor_ref,
    start_ref,
    left_ref,
    right_ref,
    panel_ref,
    cores_ref,
    high_ref,
    low_ref,
    panel_vmem,
    cores_vmem,
    out_sems,
):
    columns = factor_ref[...].T
    results = (
        (pltpu.make_async_copy(panel_vmem, panel_ref, out_sems.at[0]), panel_vmem, UP_INVERSE),
        (pltpu.make_async_copy(cores_vmem, cores_ref, out_sems.at[1]), cores_vmem, UP_PRODUCT),
    )
    def ready(n):
        for z in range(PAIRS):
            right = jnp.concatenate([tiles(right_ref[:, BASE[n] + 2 * z + p]) for p in range(2)], axis=1)
            high_ref[n, 128 * z : 128 * z + 128, :], low_ref[n, 128 * z : 128 * z + 128, :] = split(right)

    ready(0)
    ready(1)
    for n, (result, out, up) in enumerate(results):
        total = start_ref[:, 256 * n : 256 * n + 256] + dot3(left_ref, (high_ref[n], low_ref[n]))
        for i in range(2):
            fr, fi = columns[:, 2 * i : 2 * i + 1], columns[:, 2 * i + 1 : 2 * i + 2]
            by_real, by_imag = total[128 * i : 128 * i + 128], total[256 + 128 * i : 384 + 128 * i]
            real = by_real[:, :128] - by_imag[:, 128:]
            imag = by_real[:, 128:] + by_imag[:, :128]
            where = (i,) if n == 0 else (i, 0)
            out[where + (0,)] = (fr * real - fi * imag) * up
            out[where + (1,)] = (fr * imag + fi * real) * up
        result.start()
    for result, _, _ in results:
        result.wait()


def first_call(rows, right):
    vmem = pl.BlockSpec(memory_space=pltpu.VMEM)
    return pl.pallas_call(
        first_kernel,
        in_specs=[pl.BlockSpec(memory_space=pltpu.HBM), vmem],
        out_specs=(vmem, vmem, vmem),
        out_shape=(
            jax.ShapeDtypeStruct((512, 512), jnp.float32),
            jax.ShapeDtypeStruct((2, 512, 1024), jnp.bfloat16),
            jax.ShapeDtypeStruct((8, 128), jnp.float32),
        ),
        scratch_shapes=[
            pltpu.VMEM((16, ROWS + 8, 128), jnp.float32),
            pltpu.VMEM((1024, 512), jnp.bfloat16),
            pltpu.VMEM((1024, 512), jnp.bfloat16),
            pltpu.SemaphoreType.DMA((16,)),
        ],
        compiler_params=params(48),
        cost_estimate=cost(2 * 3 * 512 * 1024 * 512, 7 * 2**20),
    )(rows, right)


def second_call(factor, start, left, right):
    vmem = pl.BlockSpec(memory_space=pltpu.VMEM)
    hbm = pl.BlockSpec(memory_space=pltpu.HBM)
    shapes = (2, 2, 128, 128), (2, 1, 2, 128, 128)
    return pl.pallas_call(
        second_kernel,
        in_specs=[vmem, vmem, vmem, vmem],
        out_specs=(hbm, hbm),
        out_shape=tuple(jax.ShapeDtypeStruct(shape, jnp.float32) for shape in shapes),
        scratch_shapes=[
            pltpu.VMEM((2, 1024, 256), jnp.bfloat16),
            pltpu.VMEM((2, 1024, 256), jnp.bfloat16),
            pltpu.VMEM(shapes[0], jnp.float32),
            pltpu.VMEM(shapes[1], jnp.float32),
            pltpu.SemaphoreType.DMA((2,)),
        ],
        compiler_params=params(48),
        cost_estimate=cost(2 * 3 * 512 * 1024 * 512, 8 * 2**20),
    )(factor, start, left, right)


def spread(pairs, right):
    count = 2 * PAIRS + 2 * pairs
    got = lax.all_to_all(right[:, :count], CHIPS, 0, 0)
    return jnp.pad(got, ((0, 0), (0, right.shape[1] - count), (0, 0), (0, 0)))


def on_device(col_samples, row_samples, pivot_rows, rank_blocks, upper_inverse, upanel_left):
    f32 = jnp.float32
    vmem = pl.BlockSpec(memory_space=pltpu.VMEM)
    hbm = pl.BlockSpec(memory_space=pltpu.HBM)
    packed, sent = pl.pallas_call(
        start_kernel,
        in_specs=[hbm] * 5,
        out_specs=(hbm, hbm),
        out_shape=(jax.ShapeDtypeStruct((16, 8, 128), f32), jax.ShapeDtypeStruct((ROWS + 8, 128), f32)),
        scratch_shapes=[
            pltpu.VMEM((2, 64, 128), f32),
            pltpu.VMEM(col_samples.shape, f32),
            pltpu.VMEM(pivot_rows.shape, jnp.int32),
            pltpu.SMEM(rank_blocks.shape, jnp.int32),
            pltpu.VMEM((16, 8, 128), f32),
            pltpu.VMEM((ROWS + 8, 128), f32),
            pltpu.SemaphoreType.DMA((8,)),
        ],
        compiler_params=params(61.75),
        cost_estimate=cost(2**17, 2**18),
    )(jnp.swapaxes(upper_inverse, 1, 2), row_samples.reshape(ROWS, 128), col_samples, pivot_rows, rank_blocks)
    rows = lax.all_gather(sent, "col", axis=0)
    packed = lax.all_to_all(packed.reshape(32, 4, 128), CHIPS + ("c",), 0, 0).reshape(128, 128)
    packed = jnp.concatenate([packed[8:], packed[0:2], packed[4:8]], axis=0)
    packed = lax.all_gather(packed, "col", axis=0)
    right = pl.pallas_call(
        right_kernel,
        in_specs=[vmem, vmem],
        out_specs=vmem,
        out_shape=jax.ShapeDtypeStruct((16, 4 * PAIRS, 8, 128), f32),
        compiler_params=params(),
        cost_estimate=cost(2 * 3 * 128 * 2048 * 256, 5 * 2**20),
    )(packed, upanel_left[0])
    place = lax.axis_index("col")
    kind = (place >= 4).astype(jnp.int32) + (place >= 8).astype(jnp.int32)
    own = lax.switch(kind, [functools.partial(spread, pairs) for pairs in (2, 4, 8)], right)
    other = lax.ppermute(own, "c", [(0, 1), (1, 0)])
    start, left, factor = first_call(rows, own)
    return second_call(factor, start, left, other)


def solution(mesh):
    chips = mesh.devices.reshape(4, 4, 2, 16)
    fine = Mesh(chips, ("y", "x", "c", "col"))
    row = ("y", "x", "c")
    in_specs = (
        P(row, None, "col", None),
        P(row, None, None, "col"),
        P(row, None),
        P(row),
        P(None, "col", row),
        P("col", None, None, None),
    )
    out_specs = (P(row, None, None, "col"), P(row, "col", None, None, None))
    return jax.shard_map(
        on_device, mesh=fine, in_specs=in_specs, out_specs=out_specs, check_vma=False
    )
```
